32 devices in a mesh: fsdp: 32 (over z, y, x, core).
Axes of the slice: x: 2, y: 2, z: 4, core: 2. Of those that a mesh axis runs over, the one named last changes fastest.
Arguments:
- tokens: bfloat16 [8192, 768], P('fsdp'), may hold values from -6 to 6
- cotangent: bfloat16 [8192, 768], P('fsdp'), may hold values from -6 to 6
- counts: int32 [32], P('fsdp'), may hold values from 1 to 2, as said below
- ln1_gain: bfloat16 [768], P('fsdp'), may hold values from 0.099609375 to 1.8984375
- ln1_bias: bfloat16 [768], P('fsdp'), may hold values from -4 to 4
- w_query: bfloat16 [768, 768], P('fsdp'), may hold values from -0.3125 to 0.3125
- b_query: bfloat16 [768], P('fsdp'), may hold values from -4 to 4
- w_key: bfloat16 [768, 768], P('fsdp'), may hold values from -0.3125 to 0.3125
- w_value: bfloat16 [768, 768], P('fsdp'), may hold values from -0.21875 to 0.21875
- b_value: bfloat16 [768], P('fsdp'), may hold values from -4 to 4
- w_out: bfloat16 [768, 768], P('fsdp'), may hold values from -0.625 to 0.625
- b_out: bfloat16 [768], P('fsdp'), may hold values from -4 to 4
- ln2_gain: bfloat16 [768], P('fsdp'), may hold values from 0.099609375 to 1.8984375
- ln2_bias: bfloat16 [768], P('fsdp'), may hold values from -4 to 4
- w_fc1: bfloat16 [768, 3072], P('fsdp'), may hold values from -0.21875 to 0.21875
- b_fc1: bfloat16 [3072], P('fsdp'), may hold values from -4 to 4
- w_fc2: bfloat16 [3072, 768], P('fsdp'), may hold values from -0.15625 to 0.15625
- b_fc2: bfloat16 [768], P('fsdp'), may hold values from -4 to 4
Outputs:
- mixed: bfloat16 [8192, 768], P('fsdp')
- grad_tokens: float32 [8192, 768], P('fsdp')
- grad_ln1_gain: float32 [768], P('fsdp')
- grad_ln1_bias: float32 [768], P('fsdp')
- grad_w_query: float32 [768, 768], P('fsdp')
- grad_b_query: float32 [768], P('fsdp')
- grad_w_key: float32 [768, 768], P('fsdp')
- grad_w_value: float32 [768, 768], P('fsdp')
- grad_b_value: float32 [768], P('fsdp')
- grad_w_out: float32 [768, 768], P('fsdp')
- grad_b_out: float32 [768], P('fsdp')
- grad_ln2_gain: float32 [768], P('fsdp')
- grad_ln2_bias: float32 [768], P('fsdp')
- grad_w_fc1: float32 [768, 3072], P('fsdp')
- grad_b_fc1: float32 [3072], P('fsdp')
- grad_w_fc2: float32 [3072, 768], P('fsdp')
- grad_b_fc2: float32 [768], P('fsdp')
The draws below stay inside these ranges and needn't reach their ends.
Inputs may be any that keep to these rules, and one draw needn't show every extreme that they name: `counts`: some device has 2 live micro-batches and another has one.
All inputs are finite; a program needn't handle non-finite values.
Results may differ from the reference program's by a relative error of at most 0.013.
The reference program's roundings to bfloat16 on the way count: a program that leaves them out, or rounds other values in their place, can miss the bound.
Values may be sent and summed in bfloat16 or wider, within the bound.
A program may use at most 192 MiB of HBM per device.

```python
import math
import jax
import jax.numpy as jnp
from jax import lax

D = 768
HD = 64
FF = 3072
LENGTH = 128
SLOTS = 2
TOKENS = 8192
N_FSDP = 32


def draw_counts(key, part):
    key = jax.random.fold_in(key, 7)
    first, second, third = jax.random.split(key, 3)
    values = jax.random.randint(first, (N_FSDP,), 1, SLOTS + 1)
    fullest = jax.random.randint(second, (), 0, N_FSDP)
    emptiest = (fullest + 1 + jax.random.randint(third, (), 0, N_FSDP - 1)) % N_FSDP
    values = values.at[fullest].set(SLOTS)
    values = values.at[emptiest].set(1)
    return values.astype(jnp.int32)


def levels(own_key, dims, cuts, smallest, high):
    factor_of, own = 1.0, jax.random.fold_in(own_key, 6)
    for dim, shards_of in cuts:
        draws = jnp.exp(jax.random.uniform(jax.random.fold_in(own, dim), (shards_of,), jnp.float32, smallest / len(cuts), high / len(cuts)))
        factor_of = factor_of * jnp.repeat(draws, dims[dim] // shards_of).reshape([-1 if axis == dim else 1 for axis in range(len(dims))])
    return factor_of


def bell_draw(stream_key, extent, scale, most, cuts=(), held_as=jnp.bfloat16):
    result = jax.random.normal(stream_key, extent, jnp.float32) * scale
    if len(cuts) > 0:
        result = levels(stream_key, extent, cuts, -0.22, 0.18) * result
    return jnp.clip(result, min=-most, max=most).astype(held_as)


def setup_inputs(seed: int = 0) -> dict:
    splits = jax.random.split(jax.random.key(seed), 19)
    tokens = bell_draw(splits[0], (TOKENS, D), 1.0, 6.0, ((0, 32),))
    cotangent = bell_draw(splits[1], (TOKENS, D), 1.0, 6.0, ((0, 32),))
    counts = draw_counts(jax.random.fold_in(splits[18], 71), 0)
    ln1_gain = jnp.clip(1.0 + 0.18 * jax.random.normal(splits[3], (D,), jnp.float32), 0.099609375, 1.8984375).astype(jnp.bfloat16)
    ln1_bias = bell_draw(splits[4], (D,), 0.3, 4.0, ((0, 32),))
    w_query = bell_draw(splits[5], (D, D), (D // 2) ** -0.5, 0.3125, ((0, 32),))
    b_query = bell_draw(splits[6], (D,), 0.3, 4.0, ((0, 32),))
    w_key = bell_draw(splits[7], (D, D), (D // 2) ** -0.5, 0.3125, ((0, 32),))
    w_value = bell_draw(splits[8], (D, D), D ** -0.5, 0.21875, ((0, 32),))
    b_value = bell_draw(splits[9], (D,), 0.3, 4.0, ((0, 32),))
    w_out = bell_draw(splits[10], (D, D), (D // 8) ** -0.5, 0.625, ((0, 32),))
    b_out = bell_draw(splits[11], (D,), 0.3, 4.0, ((0, 32),))
    ln2_gain = jnp.clip(1.0 + 0.18 * jax.random.normal(splits[12], (D,), jnp.float32), 0.099609375, 1.8984375).astype(jnp.bfloat16)
    ln2_bias = bell_draw(splits[13], (D,), 0.3, 4.0, ((0, 32),))
    w_fc1 = bell_draw(splits[14], (D, FF), D ** -0.5, 0.21875, ((0, 32),))
    b_fc1 = bell_draw(splits[15], (FF,), 0.3, 4.0, ((0, 32),))
    w_fc2 = bell_draw(splits[16], (FF, D), (FF // 2) ** -0.5, 0.15625, ((0, 32),))
    b_fc2 = bell_draw(splits[17], (D,), 0.3, 4.0, ((0, 32),))
    return {"tokens": tokens, "cotangent": cotangent, "counts": counts, "ln1_gain": ln1_gain, "ln1_bias": ln1_bias, "w_query": w_query, "b_query": b_query, "w_key": w_key, "w_value": w_value, "b_value": b_value, "w_out": w_out, "b_out": b_out, "ln2_gain": ln2_gain, "ln2_bias": ln2_bias, "w_fc1": w_fc1, "b_fc1": b_fc1, "w_fc2": w_fc2, "b_fc2": b_fc2}


@jax.custom_vjp
def low(v):
    return lax.optimization_barrier(v.astype(jnp.bfloat16)).astype(jnp.float32)

@jax.custom_vjp
def low_back(v):
    return v

def low_keep(v):
    return (low(v), None)

def low_pass(kept, grad):
    return (grad,)

def back_keep(v):
    return (v, None)

def back_low(kept, grad):
    return (low(grad),)
low.defvjp(low_keep, low_pass)
low_back.defvjp(back_keep, back_low)
EPS = 1e-05
HIGH = lax.Precision.HIGHEST

def matmul(left, right):
    return jnp.einsum('bld,de->ble', left, right, precision=HIGH)

def normalize(values, gain, shift):
    center = values - lax.optimization_barrier(jnp.mean(values, -1, keepdims=True))
    spread = lax.optimization_barrier(jnp.mean(center * center, -1, keepdims=True))
    return center * lax.rsqrt(spread + EPS) * gain + shift

def layer(params, inputs):
    ln1_gain, ln1_bias, w_query, b_query, w_key, w_value, b_value, w_out, b_out, ln2_gain, ln2_bias, w_fc1, b_fc1, w_fc2, b_fc2 = params
    batch, length, width = inputs.shape
    heads = width // HD
    normed = low(normalize(inputs, ln1_gain, ln1_bias))
    queries = low_back(low(matmul(normed, w_query) + b_query)).reshape(batch, length, heads, HD)
    key_rows = low_back(low(matmul(normed, w_key))).reshape(batch, length, heads, HD)
    value_rows = low_back(low(matmul(normed, w_value) + b_value)).reshape(batch, length, heads, HD)
    scores = low_back(jnp.einsum('bqhd,bkhd->bhqk', queries, key_rows, precision=HIGH) * HD ** (-0.5))
    causal = jnp.arange(length)[:, None] >= jnp.arange(length)[None, :]
    scores = jnp.where(causal, scores, -1e+30)
    weights = low(jax.nn.softmax(scores, axis=-1))
    attended = jnp.einsum('bhqk,bkhd->bqhd', weights, value_rows, precision=HIGH).reshape(batch, length, width)
    attended = low_back(low(attended))
    branch = low_back(matmul(attended, w_out) + b_out)
    middle = inputs + branch
    normed_two = low(normalize(middle, ln2_gain, ln2_bias))
    hidden_pre = low_back(matmul(normed_two, w_fc1) + b_fc1)
    activated = low(jax.nn.gelu(hidden_pre))
    return middle + matmul(activated, w_fc2) + b_fc2

def reference(tokens, cotangent, counts, ln1_gain, ln1_bias, w_query, b_query, w_key, w_value, b_value, w_out, b_out, ln2_gain, ln2_bias, w_fc1, b_fc1, w_fc2, b_fc2):
    params = tuple((p.astype(jnp.float32) for p in (ln1_gain, ln1_bias, w_query, b_query, w_key, w_value, b_value, w_out, b_out, ln2_gain, ln2_bias, w_fc1, b_fc1, w_fc2, b_fc2)))
    width = tokens.shape[1]
    sequences = tokens.shape[0] // LENGTH
    group = math.gcd(sequences, max(1, 4096 // LENGTH))
    seq_ids = jnp.arange(sequences, dtype=jnp.int32)
    live = (seq_ids % SLOTS < counts[seq_ids // SLOTS]).astype(jnp.float32)
    live = live.reshape(sequences // group, group, 1, 1)
    inputs = tokens.astype(jnp.float32).reshape(sequences // group, group, LENGTH, width)
    grads_out = cotangent.astype(jnp.float32).reshape(sequences // group, group, LENGTH, width) * live

    def per_group(totals, pieces):
        rows, grad_rows, mask = pieces
        outputs, pullback = jax.vjp(layer, params, rows)
        grad_params, grad_inputs = pullback(grad_rows)
        totals = jax.tree.map(jnp.add, totals, grad_params)
        return (totals, (outputs * mask, grad_inputs))
    zeros = tuple((jnp.zeros(p.shape, jnp.float32) for p in params))
    totals, (outputs, grad_inputs) = lax.scan(per_group, zeros, (inputs, grads_out, live))
    mixed = outputs.reshape(tokens.shape).astype(jnp.bfloat16)
    grad_tokens = grad_inputs.reshape(tokens.shape)
    return (mixed, grad_tokens, totals[0], totals[1], totals[2], totals[3], totals[4], totals[5], totals[6], totals[7], totals[8], totals[9], totals[10], totals[11], totals[12], totals[13], totals[14])
```

```python
import jax
import jax.numpy as jnp
from jax import lax
from jax.experimental import pallas as pl
from jax.experimental.pallas import tpu as pltpu
from jax.sharding import PartitionSpec as P

HD = 64
LENGTH = 128


EPS = 1e-05
BF = jnp.bfloat16
FL = jnp.float32


def normalize(values, gain, shift):
    center = values - jnp.mean(values, -1, keepdims=True)
    spread = jnp.mean(center * center, -1, keepdims=True)
    inverse = lax.rsqrt(spread + EPS)
    plain = center * inverse
    return (plain * gain.astype(FL) + shift.astype(FL), plain, inverse)


def norm_back(grad, plain, inverse, gain):
    scaled = grad * gain.astype(FL)
    inner = (
        scaled
        - jnp.mean(scaled, -1, keepdims=True)
        - plain * jnp.mean(scaled * plain, -1, keepdims=True)
    )
    return (inverse * inner, jnp.sum(grad * plain, 0), jnp.sum(grad, 0))


def project(left, right):
    return jnp.dot(left, right, preferred_element_type=FL)


def back_project(grad, right):
    return jnp.einsum("te,de->td", grad, right, preferred_element_type=FL)


def outer_sum(left, grad):
    return jnp.einsum("td,te->de", left, grad, preferred_element_type=FL)


MESH = pl.DeviceIdType.MESH
LANES = 128
VMEM_BYTES = 50 * 1024 * 1024
OFFSETS = (0, -1, 1, -2, 2, -3, 3)


def place():
    me = lax.axis_index("fsdp")
    z = me // 8
    core = me % 2
    across_x = 2 * (1 - 2 * ((me // 2) % 2))
    across_y = 4 * (1 - 2 * ((me // 4) % 2))
    first = across_x * (1 - core) + across_y * core
    second = across_x * core + across_y * (1 - core)
    return me, z, first, second, 1 - 2 * core


def greet(me, z, first, second, sibling):
    barrier = pltpu.get_barrier_semaphore()

    def signal(device):
        pl.semaphore_signal(barrier, inc=1, device_id=(device,), device_id_type=MESH)

    signal(me + first)
    signal(me + second)
    signal(me + sibling)

    @pl.when(z > 0)
    def _():
        signal(me - 8)

    @pl.when(z < 3)
    def _():
        signal(me + 8)

    pl.semaphore_wait(barrier, 3 + (z + 3) // 4 + (6 - z) // 4)


def gather_kernel(a_ref, b_ref, all_a, all_b, sent, landed, kept):
    me, z, first, second, sibling = place()
    ring = me % 8
    pairs = ((a_ref, all_a), (b_ref, all_b))
    locals_ = [
        pltpu.make_async_copy(own, whole.at[me], kept.at[k]) for k, (own, whole) in enumerate(pairs)
    ]
    for copy in locals_:
        copy.start()
    greet(me, z, first, second, sibling)

    def copies(block, device, slot, own=False):
        return [
            pltpu.make_async_remote_copy(
                src_ref=piece if own else whole.at[block],
                dst_ref=whole.at[block],
                send_sem=sent.at[k, slot],
                recv_sem=landed.at[k, block],
                device_id=(device,),
                device_id_type=MESH,
            )
            for k, (piece, whole) in enumerate(pairs)
        ]

    def send(block, device, slot, own=False):
        for copy in copies(block, device, slot, own):
            copy.start()

    def arrive(block):
        for copy in copies(block, me, 0):
            copy.wait_recv()

    def line(step, offset, finish):
        other = z + offset
        block = me + 8 * offset
        own = offset == 0

        def act(device, slot):
            if finish:
                for copy in copies(block, device, slot, own):
                    copy.wait_send()
            else:
                send(block, device, slot, own)

        @pl.when((other >= 0) & (other <= 3))
        def _():
            if not own and not finish:
                arrive(block)
            if offset <= 0:

                @pl.when(z < 3)
                def _():
                    act(me + 8, 4 * step)

            if offset >= 0:

                @pl.when(z > 0)
                def _():
                    act(me - 8, 4 * step + 3)

            act(me + first, 4 * step + 1)
            act(me + second, 4 * step + 2)
            act(me + sibling, 28 + step)

    def across(step, offset, near, far, finish):
        other = z + offset
        block = me + 8 * offset + near * first + far * second
        base = 35 + 7 * (near + 2 * far - 1)

        @pl.when((other >= 0) & (other <= 3))
        def _():
            if not finish:
                arrive(block)
                send(block, me + sibling, base + step)
                if not far:
                    send(block, me + second, 56 + step)
            else:
                for copy in copies(block, me + sibling, base + step):
                    copy.wait_send()
                if not far:
                    for copy in copies(block, me + second, 56 + step):
                        copy.wait_send()

    for finish in (False, True):
        for step in range(len(OFFSETS) + 2):
            if step < len(OFFSETS):
                line(step, OFFSETS[step], finish)
            if 1 <= step <= len(OFFSETS):
                across(step - 1, OFFSETS[step - 1], 1, 0, finish)
                across(step - 1, OFFSETS[step - 1], 0, 1, finish)
            if step >= 2:
                across(step - 2, OFFSETS[step - 2], 1, 1, finish)
    for index in range(16):
        arrive(2 * index + (ring + sibling) % 2)
    for copy in locals_:
        copy.wait()


def gather_blocks(a, b, devices):
    if devices != 32:
        return lax.all_gather(a, "fsdp", axis=0), lax.all_gather(b, "fsdp", axis=0)
    return pl.pallas_call(
        gather_kernel,
        out_shape=(
            jax.ShapeDtypeStruct((devices,) + a.shape, a.dtype),
            jax.ShapeDtypeStruct((devices,) + b.shape, b.dtype),
        ),
        in_specs=[pl.BlockSpec(memory_space=pl.ANY)] * 2,
        out_specs=(pl.BlockSpec(memory_space=pl.ANY),) * 2,
        scratch_shapes=[
            pltpu.SemaphoreType.DMA((2, 64)),
            pltpu.SemaphoreType.DMA((2, 32)),
            pltpu.SemaphoreType.DMA((2,)),
        ],
        compiler_params=pltpu.CompilerParams(
            collective_id=0, has_side_effects=True, vmem_limit_bytes=VMEM_BYTES
        ),
    )(a, b)


def scatter_kernel(
    a_ref,
    b_ref,
    out_a,
    out_b,
    own_a,
    own_b,
    pair_a,
    pair_b,
    two_a,
    two_b,
    one_a,
    one_b,
    line_a,
    line_b,
    sent,
    landed,
    loaded,
):
    me, z, first, second, sibling = place()
    ring = me % 8
    whole = (a_ref, b_ref)
    own, pair = (own_a, own_b), (pair_a, pair_b)
    two, one, lane = (two_a, two_b), (one_a, one_b), (line_a, line_b)
    final = (out_a, out_b)

    def slot16(block):
        return block // 2

    def targets():
        for a, b in ((1, 1), (0, 1), (1, 0), (0, 0)):
            for to in range(4):
                yield to, a, b

    loads = []
    for order, (to, a, b) in enumerate(targets()):
        block = 8 * to + ring + a * first + b * second
        for k in range(2):
            copy = pltpu.make_async_copy(
                whole[k].at[block], own[k].at[slot16(block)], loaded.at[k, order]
            )
            copy.start()
            loads.append(copy)
    greet(me, z, first, second, sibling)

    def remote(source, target, k, out_slot, in_slot, device):
        return pltpu.make_async_remote_copy(
            src_ref=source,
            dst_ref=target,
            send_sem=sent.at[k, out_slot],
            recv_sem=landed.at[k, in_slot],
            device_id=(device,),
            device_id_type=MESH,
        )

    def pair_copy(order, to, a, b, k):
        block = 8 * to + (ring + sibling) + b * first + a * second
        return remote(
            whole[k].at[block], pair[k].at[slot16(block)], k, order, slot16(block), me + sibling
        )

    for order, (to, a, b) in enumerate(targets()):
        for k in range(2):
            pair_copy(order, to, a, b, k).start()

    def add(k, target, sources):
        if k == 0:
            wide = target.shape[-1]
            chunk = LANES * max(d for d in range(1, 9) if (wide // LANES) % d == 0)

            @pl.loop(0, wide // chunk)
            def _(i):
                part = pl.ds(pl.multiple_of(i * chunk, LANES), chunk)
                total = sources[0][:, part].astype(FL)
                for source in sources[1:]:
                    total = total + source[:, part].astype(FL)
                target[:, part] = total.astype(target.dtype)
        else:
            chunk = 16

            @pl.loop(0, target.shape[0] // chunk)
            def _(i):
                part = pl.ds(pl.multiple_of(i * chunk, chunk), chunk)
                total = sources[0][part, :].astype(FL)
                for source in sources[1:]:
                    total = total + source[part, :].astype(FL)
                target[part, :] = total.astype(target.dtype)

    def base(order, to, a, b, k):
        block = 8 * to + ring + a * first + b * second
        slot = slot16(block)
        loads[2 * order + k].wait()
        remote(whole[k].at[block], pair[k].at[slot], k, 0, slot, me).wait_recv()
        return own[k].at[slot], pair[k].at[slot]

    def second_copy(to, a, k, source):
        return remote(source, two[k].at[2 * to + a], k, 16 + 2 * to + a, 16 + 2 * to + a, me + second)

    def first_copy(to, k, source):
        return remote(source, one[k].at[to], k, 24 + to, 24 + to, me + first)

    orders = list(targets())
    for order, (to, a, b) in enumerate(orders[:8]):
        for k in range(2):
            mine, theirs = base(order, to, a, b, k)
            add(k, mine, (mine, theirs))
            second_copy(to, a, k, mine).start()
    for order in range(8, 12):
        to, a, b = orders[order]
        for k in range(2):
            mine, theirs = base(order, to, a, b, k)
            second_copy(to, a, k, mine).wait_recv()
            add(k, mine, (mine, theirs, two[k].at[2 * to + a]))
            first_copy(to, k, mine).start()
    for order in range(12, 16):
        to, a, b = orders[order]
        for k in range(2):
            mine, theirs = base(order, to, a, b, k)
            second_copy(to, a, k, mine).wait_recv()
            first_copy(to, k, mine).wait_recv()
            add(k, mine, (mine, theirs, two[k].at[2 * to + a], one[k].at[to]))

    def along(goal, k, upward):
        slot = 28 + goal + (0 if upward else 4)
        place_in = goal + (0 if upward else 4)
        mine = own[k].at[slot16(8 * goal + ring)]
        return mine, remote(
            mine, lane[k].at[place_in], k, slot, slot, me + 8 if upward else me - 8
        )

    for goal in (3, 2, 1):
        for k in range(2):
            mine, copy = along(goal, k, True)

            @pl.when(z < goal)
            def _():
                @pl.when(z > 0)
                def _():
                    copy.wait_recv()
                    add(k, mine, (mine, lane[k].at[goal]))

                copy.start()

            down = 3 - goal
            mine_down, copy_down = along(down, k, False)

            @pl.when(z > down)
            def _():
                @pl.when(z < 3)
                def _():
                    copy_down.wait_recv()
                    add(k, mine_down, (mine_down, lane[k].at[4 + down]))

                copy_down.start()

    for goal in range(4):

        @pl.when(z == goal)
        def _():
            for k in range(2):
                mine = own[k].at[slot16(8 * goal + ring)]
                sources = [mine]
                if goal > 0:
                    along(goal, k, True)[1].wait_recv()
                    sources.append(lane[k].at[goal])
                if goal < 3:
                    along(goal, k, False)[1].wait_recv()
                    sources.append(lane[k].at[4 + goal])
                add(k, final[k], sources)

    for order, (to, a, b) in enumerate(orders):
        for k in range(2):
            pair_copy(order, to, a, b, k).wait_send()
            mine = own[k].at[0]
            if order < 8:
                second_copy(to, a, k, mine).wait_send()
            elif order < 12:
                first_copy(to, k, mine).wait_send()
    for goal in range(4):
        for k in range(2):

            @pl.when(z < goal)
            def _():
                along(goal, k, True)[1].wait_send()

            @pl.when(z > goal)
            def _():
                along(goal, k, False)[1].wait_send()


def scatter_blocks(a, b, devices):
    if devices != 32:
        return (
            lax.psum_scatter(a.astype(FL), "fsdp", scatter_dimension=0),
            lax.psum_scatter(b.astype(FL), "fsdp", scatter_dimension=0),
        )
    vmem = pl.BlockSpec(memory_space=pltpu.VMEM)
    scratch = []
    for count in (16, 16, 8, 4, 8):
        scratch.append(pltpu.VMEM((count,) + a.shape[1:], BF))
        scratch.append(pltpu.VMEM((count,) + b.shape[1:], BF))
    return pl.pallas_call(
        scatter_kernel,
        out_shape=(
            jax.ShapeDtypeStruct(a.shape[1:], FL),
            jax.ShapeDtypeStruct(b.shape[1:], FL),
        ),
        in_specs=[pl.BlockSpec(memory_space=pl.ANY)] * 2,
        out_specs=(vmem, vmem),
        scratch_shapes=scratch
        + [
            pltpu.SemaphoreType.DMA((2, 36)),
            pltpu.SemaphoreType.DMA((2, 36)),
            pltpu.SemaphoreType.DMA((2, 16)),
        ],
        compiler_params=pltpu.CompilerParams(
            collective_id=1, has_side_effects=True, vmem_limit_bytes=VMEM_BYTES
        ),
    )(a, b)


def column_sums(values):
    return jnp.sum(values, 0)


def on_device(
    tokens,
    cotangent,
    counts,
    ln1_gain,
    ln1_bias,
    w_query,
    b_query,
    w_key,
    w_value,
    b_value,
    w_out,
    b_out,
    ln2_gain,
    ln2_bias,
    w_fc1,
    b_fc1,
    w_fc2,
    b_fc2,
):
    devices = lax.axis_size("fsdp")
    rows, width = tokens.shape
    slots = rows // LENGTH
    heads = width // HD
    depth = w_query.shape[0]
    hidden = w_fc1.shape[1]
    wide = 4 * width + hidden

    vectors = (ln1_gain, ln1_bias, b_query, b_value, b_out, ln2_gain, ln2_bias, b_fc2)
    few = len(vectors)
    per_row = b_fc1.shape[0] // depth
    small = jnp.concatenate(
        [jnp.stack(vectors, 1), b_fc1.reshape(depth, per_row)], axis=1
    )
    small = jnp.pad(small, ((0, 0), (0, LANES - small.shape[1])))
    block_a = jnp.concatenate([w_query, w_key, w_value, w_out, w_fc1, small], axis=1)
    all_a, all_b = gather_blocks(block_a, w_fc2, devices)
    all_a = all_a.reshape(width, wide + LANES)
    w_in = all_a[:, : 3 * width]
    w_out = all_a[:, 3 * width : 4 * width]
    w_fc1 = all_a[:, 4 * width : wide]
    w_fc2 = all_b.reshape(hidden, width)
    small = all_a[:, wide : wide + few + per_row].astype(FL)
    ln1_gain, ln1_bias, b_query, b_value, b_out, ln2_gain, ln2_bias, b_fc2 = small[:, :few].T
    b_fc1 = small[:, few:].reshape(hidden)

    live = (jnp.arange(rows, dtype=jnp.int32) // LENGTH < counts[0]).astype(FL)[:, None]
    inputs = tokens.astype(FL)
    normed_full, plain_one, inverse_one = normalize(inputs, ln1_gain, ln1_bias)
    normed = normed_full.astype(BF)
    b_in = jnp.concatenate([b_query, jnp.zeros_like(b_query), b_value])
    in_rows = (project(normed, w_in) + b_in).astype(BF)

    def split(values):
        return values.reshape(slots, LENGTH, heads, HD)

    queries = split(in_rows[:, :width])
    key_rows = split(in_rows[:, width : 2 * width])
    value_rows = split(in_rows[:, 2 * width :])
    scores = jnp.einsum("bqhd,bkhd->bhqk", queries, key_rows, preferred_element_type=FL)
    scores = scores * HD ** (-0.5)
    causal = jnp.arange(LENGTH)[:, None] >= jnp.arange(LENGTH)[None, :]
    scores = jnp.where(causal, scores, -1e30)
    highest = jnp.max(scores, -1, keepdims=True)
    expo = jnp.exp(scores - highest)
    probs = expo / jnp.sum(expo, -1, keepdims=True)
    weights = probs.astype(BF)
    attended = jnp.einsum("bhqk,bkhd->bqhd", weights, value_rows, preferred_element_type=FL)
    attended = attended.reshape(rows, width).astype(BF)
    middle = inputs + project(attended, w_out) + b_out
    normed_two_full, plain_two, inverse_two = normalize(middle, ln2_gain, ln2_bias)
    normed_two = normed_two_full.astype(BF)
    hidden_pre = project(normed_two, w_fc1) + b_fc1
    gelu, gelu_pull = jax.vjp(jax.nn.gelu, hidden_pre)
    activated = gelu.astype(BF)
    mixed = (live * (middle + project(activated, w_fc2) + b_fc2)).astype(BF)

    grad_out = cotangent.astype(FL) * live
    grad_rows = grad_out.astype(BF)
    grad_w_fc2 = outer_sum(activated, grad_rows)
    grad_act = back_project(grad_rows, w_fc2)
    grad_pre = gelu_pull(grad_act)[0].astype(BF)
    grad_w_fc1 = outer_sum(normed_two, grad_pre)
    grad_norm_two = back_project(grad_pre, w_fc1)
    through_two, grad_ln2_gain, grad_ln2_bias = norm_back(
        grad_norm_two, plain_two, inverse_two, ln2_gain
    )
    grad_middle = grad_out + through_two
    grad_branch = grad_middle.astype(BF)
    grad_w_out = outer_sum(attended, grad_branch)
    grad_att = split(back_project(grad_branch, w_out).astype(BF))
    grad_probs = jnp.einsum("bqhd,bkhd->bhqk", grad_att, value_rows, preferred_element_type=FL)
    grad_values = jnp.einsum("bhqk,bqhd->bkhd", weights, grad_att, preferred_element_type=FL)
    grad_scores = probs * (grad_probs - jnp.sum(probs * grad_probs, -1, keepdims=True))
    grad_scores = grad_scores.astype(BF)
    grad_queries = jnp.einsum("bhqk,bkhd->bqhd", grad_scores, key_rows, preferred_element_type=FL)
    grad_keys = jnp.einsum("bhqk,bqhd->bkhd", grad_scores, queries, preferred_element_type=FL)
    grad_in = jnp.concatenate(
        [
            (grad_queries * HD ** (-0.5)).astype(BF).reshape(rows, width),
            (grad_keys * HD ** (-0.5)).astype(BF).reshape(rows, width),
            grad_values.astype(BF).reshape(rows, width),
        ],
        axis=1,
    )
    grad_w_in = outer_sum(normed, grad_in)
    grad_norm_one = back_project(grad_in, w_in)
    through_one, grad_ln1_gain, grad_ln1_bias = norm_back(
        grad_norm_one, plain_one, inverse_one, ln1_gain
    )
    grad_tokens = grad_middle + through_one

    in_sums = column_sums(grad_in.astype(FL))
    vectors = (
        grad_ln1_gain,
        grad_ln1_bias,
        in_sums[:width],
        in_sums[2 * width :],
        column_sums(grad_branch.astype(FL)),
        grad_ln2_gain,
        grad_ln2_bias,
        column_sums(grad_out),
    )
    small = jnp.concatenate(
        [jnp.stack(vectors, 1), column_sums(grad_pre.astype(FL)).reshape(width, per_row)], axis=1
    )
    small = jnp.pad(small, ((0, 0), (0, LANES - small.shape[1])))
    sums_a = jnp.concatenate(
        [grad_w_in.astype(BF), grad_w_out.astype(BF), grad_w_fc1.astype(BF), small.astype(BF)],
        axis=1,
    )
    got_a, got_b = scatter_blocks(
        sums_a.reshape(devices, depth, wide + LANES),
        grad_w_fc2.astype(BF).reshape((devices,) + (hidden // devices, width)),
        devices,
    )
    small = got_a[:, wide : wide + few + per_row]
    columns = tuple(small[:, i] for i in range(few))
    return (
        mixed,
        grad_tokens,
        columns[0],
        columns[1],
        got_a[:, :width],
        columns[2],
        got_a[:, width : 2 * width],
        got_a[:, 2 * width : 3 * width],
        columns[3],
        got_a[:, 3 * width : 4 * width],
        columns[4],
        columns[5],
        columns[6],
        got_a[:, 4 * width : wide],
        small[:, few:].reshape(hidden // devices),
        got_b,
        columns[7],
    )


def solution(mesh):
    in_specs = (
        P("fsdp", None),
        P("fsdp", None),
        P("fsdp"),
        P("fsdp"),
        P("fsdp"),
        P("fsdp", None),
        P("fsdp"),
        P("fsdp", None),
        P("fsdp", None),
        P("fsdp"),
        P("fsdp", None),
        P("fsdp"),
        P("fsdp"),
        P("fsdp"),
        P("fsdp", None),
        P("fsdp"),
        P("fsdp", None),
        P("fsdp"),
    )
    out_specs = (
        P("fsdp", None),
        P("fsdp", None),
        P("fsdp"),
        P("fsdp"),
        P("fsdp", None),
        P("fsdp"),
        P("fsdp", None),
        P("fsdp", None),
        P("fsdp"),
        P("fsdp", None),
        P("fsdp"),
        P("fsdp"),
        P("fsdp"),
        P("fsdp", None),
        P("fsdp"),
        P("fsdp", None),
        P("fsdp"),
    )
    return jax.shard_map(
        on_device, mesh=mesh, in_specs=in_specs, out_specs=out_specs, check_vma=False
    )
```

```python
import jax
import jax.numpy as jnp
from jax import lax
from jax.experimental import pallas as pl
from jax.experimental.pallas import tpu as pltpu
from jax.sharding import PartitionSpec as P

HD = 64
LENGTH = 128


EPS = 1e-05
BF = jnp.bfloat16
FL = jnp.float32


def normalize(values, gain, shift):
    center = values - jnp.mean(values, -1, keepdims=True)
    spread = jnp.mean(center * center, -1, keepdims=True)
    inverse = lax.rsqrt(spread + EPS)
    plain = center * inverse
    return (plain * gain.astype(FL) + shift.astype(FL), plain, inverse)


def norm_back(grad, plain, inverse, gain):
    scaled = grad * gain.astype(FL)
    inner = (
        scaled
        - jnp.mean(scaled, -1, keepdims=True)
        - plain * jnp.mean(scaled * plain, -1, keepdims=True)
    )
    return (inverse * inner, jnp.sum(grad * plain, 0), jnp.sum(grad, 0))


def project(left, right):
    return jnp.dot(left, right, preferred_element_type=FL)


def back_project(grad, right):
    return jnp.einsum("te,de->td", grad, right, preferred_element_type=FL)


def outer_sum(left, grad):
    return jnp.einsum("td,te->de", left, grad, preferred_element_type=FL)


MESH = pl.DeviceIdType.MESH
LANES = 128
VMEM_BYTES = 50 * 1024 * 1024
OFFSETS = (0, -1, 1, -2, 2, -3, 3)


def place():
    me = lax.axis_index("fsdp")
    z = me // 8
    core = me % 2
    across_x = 2 * (1 - 2 * ((me // 2) % 2))
    across_y = 4 * (1 - 2 * ((me // 4) % 2))
    first = across_x * (1 - core) + across_y * core
    second = across_x * core + across_y * (1 - core)
    return me, z, first, second, 1 - 2 * core


def greet(me, z, first, second, sibling):
    barrier = pltpu.get_barrier_semaphore()

    def signal(device):
        pl.semaphore_signal(barrier, inc=1, device_id=(device,), device_id_type=MESH)

    signal(me + first)
    signal(me + second)
    signal(me + sibling)

    @pl.when(z > 0)
    def _():
        signal(me - 8)

    @pl.when(z < 3)
    def _():
        signal(me + 8)

    pl.semaphore_wait(barrier, 3 + (z + 3) // 4 + (6 - z) // 4)


def gather_kernel(a_ref, b_ref, all_a, all_b, sent, landed, kept):
    me, z, first, second, sibling = place()
    ring = me % 8
    pairs = ((a_ref, all_a), (b_ref, all_b))
    locals_ = [
        pltpu.make_async_copy(own, whole.at[me], kept.at[k]) for k, (own, whole) in enumerate(pairs)
    ]
    for copy in locals_:
        copy.start()
    greet(me, z, first, second, sibling)

    def copies(block, device, slot, own=False, only=(0, 1)):
        return [
            pltpu.make_async_remote_copy(
                src_ref=piece if own else whole.at[block],
                dst_ref=whole.at[block],
                send_sem=sent.at[k, slot],
                recv_sem=landed.at[k, block],
                device_id=(device,),
                device_id_type=MESH,
            )
            for k, (piece, whole) in enumerate(pairs)
            if k in only
        ]

    def send(block, device, slot, own=False, only=(0, 1)):
        for copy in copies(block, device, slot, own, only):
            copy.start()

    def arrive(block, only=(0, 1)):
        for copy in copies(block, me, 0, only=only):
            copy.wait_recv()

    def line(step, offset, finish):
        other = z + offset
        block = me + 8 * offset
        own = offset == 0

        def act(device, slot, k):
            if finish:
                for copy in copies(block, device, slot, own, (k,)):
                    copy.wait_send()
            else:
                send(block, device, slot, own, (k,))

        @pl.when((other >= 0) & (other <= 3))
        def _():
            for k in range(2):
                if not own and not finish:
                    arrive(block, (k,))
                if offset <= 0:

                    @pl.when(z < 3)
                    def _():
                        act(me + 8, 4 * step, k)

                if offset >= 0:

                    @pl.when(z > 0)
                    def _():
                        act(me - 8, 4 * step + 3, k)

                act(me + first, 4 * step + 1, k)
                act(me + second, 4 * step + 2, k)
                act(me + sibling, 28 + step, k)

    def across(step, offset, near, far, finish):
        other = z + offset
        block = me + 8 * offset + near * first + far * second
        base = 35 + 7 * (near + 2 * far - 1)

        @pl.when((other >= 0) & (other <= 3))
        def _():
            for k in range(2):
                if not finish:
                    arrive(block, (k,))
                    if not far:
                        send(block, me + second, 56 + step, only=(k,))
                    send(block, me + sibling, base + step, only=(k,))
                else:
                    for copy in copies(block, me + sibling, base + step, only=(k,)):
                        copy.wait_send()
                    if not far:
                        for copy in copies(block, me + second, 56 + step, only=(k,)):
                            copy.wait_send()

    for finish in (False, True):
        for step in range(len(OFFSETS) + 2):
            if step < len(OFFSETS):
                line(step, OFFSETS[step], finish)
            if 1 <= step <= len(OFFSETS):
                across(step - 1, OFFSETS[step - 1], 1, 0, finish)
                across(step - 1, OFFSETS[step - 1], 0, 1, finish)
            if step >= 2:
                across(step - 2, OFFSETS[step - 2], 1, 1, finish)
    for index in range(16):
        arrive(2 * index + (ring + sibling) % 2)
    for copy in locals_:
        copy.wait()


def gather_blocks(a, b, devices):
    if devices != 32:
        return lax.all_gather(a, "fsdp", axis=0), lax.all_gather(b, "fsdp", axis=0)
    return pl.pallas_call(
        gather_kernel,
        out_shape=(
            jax.ShapeDtypeStruct((devices,) + a.shape, a.dtype),
            jax.ShapeDtypeStruct((devices,) + b.shape, b.dtype),
        ),
        in_specs=[pl.BlockSpec(memory_space=pl.ANY)] * 2,
        out_specs=(pl.BlockSpec(memory_space=pl.ANY),) * 2,
        scratch_shapes=[
            pltpu.SemaphoreType.DMA((2, 64)),
            pltpu.SemaphoreType.DMA((2, 32)),
            pltpu.SemaphoreType.DMA((2,)),
        ],
        compiler_params=pltpu.CompilerParams(
            collective_id=0, has_side_effects=True, vmem_limit_bytes=VMEM_BYTES
        ),
    )(a, b)


def scatter_kernel(
    a_ref,
    b_ref,
    out_a,
    out_b,
    own_a,
    own_b,
    pair_a,
    pair_b,
    two_a,
    two_b,
    one_a,
    one_b,
    line_a,
    line_b,
    sent,
    landed,
    loaded,
):
    me, z, first, second, sibling = place()
    ring = me % 8
    whole = (a_ref, b_ref)
    own, pair = (own_a, own_b), (pair_a, pair_b)
    two, one, lane = (two_a, two_b), (one_a, one_b), (line_a, line_b)
    final = (out_a, out_b)

    def slot16(block):
        return block // 2

    half = z // 2
    goals = (3 - 3 * half, 2 - half, z + 1 - 2 * (z % 2), z)
    kinds = ((1, 1), (0, 1), (1, 0), (0, 0))
    orders = [(to, a, b) for to in goals for a, b in kinds]

    loads = []
    for order, (to, a, b) in enumerate(orders):
        block = 8 * to + ring + a * first + b * second
        for k in range(2):
            copy = pltpu.make_async_copy(
                whole[k].at[block], own[k].at[slot16(block)], loaded.at[k, order]
            )
            copy.start()
            loads.append(copy)
    greet(me, z, first, second, sibling)

    def remote(source, target, k, out_slot, in_slot, device):
        return pltpu.make_async_remote_copy(
            src_ref=source,
            dst_ref=target,
            send_sem=sent.at[k, out_slot],
            recv_sem=landed.at[k, in_slot],
            device_id=(device,),
            device_id_type=MESH,
        )

    def pair_copy(order, to, a, b, k):
        block = 8 * to + (ring + sibling) + b * first + a * second
        return remote(
            whole[k].at[block], pair[k].at[slot16(block)], k, order, slot16(block), me + sibling
        )

    for order, (to, a, b) in enumerate(orders):
        for k in range(2):
            pair_copy(order, to, a, b, k).start()

    def add(k, target, sources):
        if k == 0:
            wide = target.shape[-1]
            chunk = LANES * max(d for d in range(1, 9) if (wide // LANES) % d == 0)

            @pl.loop(0, wide // chunk)
            def _(i):
                part = pl.ds(pl.multiple_of(i * chunk, LANES), chunk)
                total = sources[0][:, part].astype(FL)
                for source in sources[1:]:
                    total = total + source[:, part].astype(FL)
                target[:, part] = total.astype(target.dtype)
        else:
            chunk = 16

            @pl.loop(0, target.shape[0] // chunk)
            def _(i):
                part = pl.ds(pl.multiple_of(i * chunk, chunk), chunk)
                total = sources[0][part, :].astype(FL)
                for source in sources[1:]:
                    total = total + source[part, :].astype(FL)
                target[part, :] = total.astype(target.dtype)

    def base(order, to, a, b, k):
        block = 8 * to + ring + a * first + b * second
        slot = slot16(block)
        loads[2 * order + k].wait()
        remote(whole[k].at[block], pair[k].at[slot], k, 0, slot, me).wait_recv()
        return own[k].at[slot], pair[k].at[slot]

    def second_copy(to, a, k, source):
        return remote(source, two[k].at[2 * to + a], k, 16 + 2 * to + a, 16 + 2 * to + a, me + second)

    def first_copy(to, k, source):
        return remote(source, one[k].at[to], k, 24 + to, 24 + to, me + first)

    def along(goal, k, upward):
        slot = goal + (0 if upward else 4)
        mine = own[k].at[slot16(8 * goal + ring)]
        return remote(
            mine, lane[k].at[slot], k, 28 + slot, 28 + slot, me + 8 if upward else me - 8
        )

    def to_second(step):
        for kind in (0, 1):
            to, a, b = orders[4 * step + kind]
            for k in range(2):
                mine, theirs = base(4 * step + kind, to, a, b, k)
                add(k, mine, (mine, theirs))
                second_copy(to, a, k, mine).start()

    def to_first(step):
        to, a, b = orders[4 * step + 2]
        for k in range(2):
            mine, theirs = base(4 * step + 2, to, a, b, k)
            second_copy(to, a, k, mine).wait_recv()
            add(k, mine, (mine, theirs, two[k].at[2 * to + a]))
            first_copy(to, k, mine).start()

    def to_line(step):
        to, a, b = orders[4 * step + 3]
        for k in range(2):
            mine, theirs = base(4 * step + 3, to, a, b, k)
            second_copy(to, a, k, mine).wait_recv()
            first_copy(to, k, mine).wait_recv()
            sources = (mine, theirs, two[k].at[2 * to + a], one[k].at[to])
            up, down = along(to, k, True), along(to, k, False)
            from_below, from_above = lane[k].at[to], lane[k].at[4 + to]
            if step == 3:

                @pl.when(z == 0)
                def _():
                    down.wait_recv()
                    add(k, final[k], sources + (from_above,))

                @pl.when(z == 3)
                def _():
                    up.wait_recv()
                    add(k, final[k], sources + (from_below,))

                @pl.when((z > 0) & (z < 3))
                def _():
                    up.wait_recv()
                    down.wait_recv()
                    add(k, final[k], sources + (from_below, from_above))

                continue

            @pl.when(to > z)
            def _():
                @pl.when(z > 0)
                def _():
                    up.wait_recv()
                    add(k, mine, sources + (from_below,))

                @pl.when(z == 0)
                def _():
                    add(k, mine, sources)

                up.start()

            @pl.when(to < z)
            def _():
                @pl.when(z < 3)
                def _():
                    down.wait_recv()
                    add(k, mine, sources + (from_above,))

                @pl.when(z == 3)
                def _():
                    add(k, mine, sources)

                down.start()

    to_second(0)
    to_second(1)
    to_second(2)
    to_first(0)
    to_second(3)
    to_first(1)
    to_line(0)
    to_first(2)
    to_line(1)
    to_first(3)
    to_line(2)
    to_line(3)

    for order, (to, a, b) in enumerate(orders):
        for k in range(2):
            pair_copy(order, to, a, b, k).wait_send()
            mine = own[k].at[0]
            if b == 1:
                second_copy(to, a, k, mine).wait_send()
            elif a == 1:
                first_copy(to, k, mine).wait_send()
            elif order < 12:

                @pl.when(to > z)
                def _():
                    along(to, k, True).wait_send()

                @pl.when(to < z)
                def _():
                    along(to, k, False).wait_send()


def scatter_blocks(a, b, devices):
    if devices != 32:
        return (
            lax.psum_scatter(a.astype(FL), "fsdp", scatter_dimension=0),
            lax.psum_scatter(b.astype(FL), "fsdp", scatter_dimension=0),
        )
    vmem = pl.BlockSpec(memory_space=pltpu.VMEM)
    scratch = []
    for count in (16, 16, 8, 4, 8):
        scratch.append(pltpu.VMEM((count,) + a.shape[1:], BF))
        scratch.append(pltpu.VMEM((count,) + b.shape[1:], BF))
    return pl.pallas_call(
        scatter_kernel,
        out_shape=(
            jax.ShapeDtypeStruct(a.shape[1:], FL),
            jax.ShapeDtypeStruct(b.shape[1:], FL),
        ),
        in_specs=[pl.BlockSpec(memory_space=pl.ANY)] * 2,
        out_specs=(vmem, vmem),
        scratch_shapes=scratch
        + [
            pltpu.SemaphoreType.DMA((2, 36)),
            pltpu.SemaphoreType.DMA((2, 36)),
            pltpu.SemaphoreType.DMA((2, 16)),
        ],
        compiler_params=pltpu.CompilerParams(
            collective_id=1, has_side_effects=True, vmem_limit_bytes=VMEM_BYTES
        ),
    )(a, b)


def column_sums(values):
    return jnp.sum(values, 0)


def on_device(
    tokens,
    cotangent,
    counts,
    ln1_gain,
    ln1_bias,
    w_query,
    b_query,
    w_key,
    w_value,
    b_value,
    w_out,
    b_out,
    ln2_gain,
    ln2_bias,
    w_fc1,
    b_fc1,
    w_fc2,
    b_fc2,
):
    devices = lax.axis_size("fsdp")
    rows, width = tokens.shape
    slots = rows // LENGTH
    heads = width // HD
    depth = w_query.shape[0]
    hidden = w_fc1.shape[1]
    wide = 4 * width + hidden

    vectors = (ln1_gain, ln1_bias, b_query, b_value, b_out, ln2_gain, ln2_bias, b_fc2)
    few = len(vectors)
    per_row = b_fc1.shape[0] // depth
    small = jnp.concatenate(
        [jnp.stack(vectors, 1), b_fc1.reshape(depth, per_row)], axis=1
    )
    small = jnp.pad(small, ((0, 0), (0, LANES - small.shape[1])))
    block_a = jnp.concatenate([w_query, w_key, w_value, w_out, w_fc1, small], axis=1)
    all_a, all_b = gather_blocks(block_a, w_fc2, devices)
    all_a = all_a.reshape(width, wide + LANES)
    w_in = all_a[:, : 3 * width]
    w_out = all_a[:, 3 * width : 4 * width]
    w_fc1 = all_a[:, 4 * width : wide]
    w_fc2 = all_b.reshape(hidden, width)
    small = all_a[:, wide : wide + few + per_row].astype(FL)
    ln1_gain, ln1_bias, b_query, b_value, b_out, ln2_gain, ln2_bias, b_fc2 = small[:, :few].T
    b_fc1 = small[:, few:].reshape(hidden)

    live = (jnp.arange(rows, dtype=jnp.int32) // LENGTH < counts[0]).astype(FL)[:, None]
    inputs = tokens.astype(FL)
    normed_full, plain_one, inverse_one = normalize(inputs, ln1_gain, ln1_bias)
    normed = normed_full.astype(BF)
    b_in = jnp.concatenate([b_query, jnp.zeros_like(b_query), b_value])
    in_rows = (project(normed, w_in) + b_in).astype(BF)

    def split(values):
        return values.reshape(slots, LENGTH, heads, HD)

    queries = split(in_rows[:, :width])
    key_rows = split(in_rows[:, width : 2 * width])
    value_rows = split(in_rows[:, 2 * width :])
    scores = jnp.einsum("bqhd,bkhd->bhqk", queries, key_rows, preferred_element_type=FL)
    scores = scores * HD ** (-0.5)
    causal = jnp.arange(LENGTH)[:, None] >= jnp.arange(LENGTH)[None, :]
    scores = jnp.where(causal, scores, -1e30)
    highest = jnp.max(scores, -1, keepdims=True)
    expo = jnp.exp(scores - highest)
    probs = expo / jnp.sum(expo, -1, keepdims=True)
    weights = probs.astype(BF)
    attended = jnp.einsum("bhqk,bkhd->bqhd", weights, value_rows, preferred_element_type=FL)
    attended = attended.reshape(rows, width).astype(BF)
    middle = inputs + project(attended, w_out) + b_out
    normed_two_full, plain_two, inverse_two = normalize(middle, ln2_gain, ln2_bias)
    normed_two = normed_two_full.astype(BF)
    hidden_pre = project(normed_two, w_fc1) + b_fc1
    gelu, gelu_pull = jax.vjp(jax.nn.gelu, hidden_pre)
    activated = gelu.astype(BF)
    mixed = (live * (middle + project(activated, w_fc2) + b_fc2)).astype(BF)

    grad_out = cotangent.astype(FL) * live
    grad_rows = grad_out.astype(BF)
    grad_w_fc2 = outer_sum(activated, grad_rows)
    grad_act = back_project(grad_rows, w_fc2)
    grad_pre = gelu_pull(grad_act)[0].astype(BF)
    grad_w_fc1 = outer_sum(normed_two, grad_pre)
    grad_norm_two = back_project(grad_pre, w_fc1)
    through_two, grad_ln2_gain, grad_ln2_bias = norm_back(
        grad_norm_two, plain_two, inverse_two, ln2_gain
    )
    grad_middle = grad_out + through_two
    grad_branch = grad_middle.astype(BF)
    grad_w_out = outer_sum(attended, grad_branch)
    grad_att = split(back_project(grad_branch, w_out).astype(BF))
    grad_probs = jnp.einsum("bqhd,bkhd->bhqk", grad_att, value_rows, preferred_element_type=FL)
    grad_values = jnp.einsum("bhqk,bqhd->bkhd", weights, grad_att, preferred_element_type=FL)
    grad_scores = probs * (grad_probs - jnp.sum(probs * grad_probs, -1, keepdims=True))
    grad_scores = grad_scores.astype(BF)
    grad_queries = jnp.einsum("bhqk,bkhd->bqhd", grad_scores, key_rows, preferred_element_type=FL)
    grad_keys = jnp.einsum("bhqk,bqhd->bkhd", grad_scores, queries, preferred_element_type=FL)
    grad_in = jnp.concatenate(
        [
            (grad_queries * HD ** (-0.5)).astype(BF).reshape(rows, width),
            (grad_keys * HD ** (-0.5)).astype(BF).reshape(rows, width),
            grad_values.astype(BF).reshape(rows, width),
        ],
        axis=1,
    )
    grad_w_in = outer_sum(normed, grad_in)
    grad_norm_one = back_project(grad_in, w_in)
    through_one, grad_ln1_gain, grad_ln1_bias = norm_back(
        grad_norm_one, plain_one, inverse_one, ln1_gain
    )
    grad_tokens = grad_middle + through_one

    in_sums = column_sums(grad_in.astype(FL))
    vectors = (
        grad_ln1_gain,
        grad_ln1_bias,
        in_sums[:width],
        in_sums[2 * width :],
        column_sums(grad_branch.astype(FL)),
        grad_ln2_gain,
        grad_ln2_bias,
        column_sums(grad_out),
    )
    small = jnp.concatenate(
        [jnp.stack(vectors, 1), column_sums(grad_pre.astype(FL)).reshape(width, per_row)], axis=1
    )
    small = jnp.pad(small, ((0, 0), (0, LANES - small.shape[1])))
    sums_a = jnp.concatenate(
        [grad_w_in.astype(BF), grad_w_out.astype(BF), grad_w_fc1.astype(BF), small.astype(BF)],
        axis=1,
    )
    got_a, got_b = scatter_blocks(
        sums_a.reshape(devices, depth, wide + LANES),
        grad_w_fc2.astype(BF).reshape((devices,) + (hidden // devices, width)),
        devices,
    )
    small = got_a[:, wide : wide + few + per_row]
    columns = tuple(small[:, i] for i in range(few))
    return (
        mixed,
        grad_tokens,
        columns[0],
        columns[1],
        got_a[:, :width],
        columns[2],
        got_a[:, width : 2 * width],
        got_a[:, 2 * width : 3 * width],
        columns[3],
        got_a[:, 3 * width : 4 * width],
        columns[4],
        columns[5],
        columns[6],
        got_a[:, 4 * width : wide],
        small[:, few:].reshape(hidden // devices),
        got_b,
        columns[7],
    )


def solution(mesh):
    in_specs = (
        P("fsdp", None),
        P("fsdp", None),
        P("fsdp"),
        P("fsdp"),
        P("fsdp"),
        P("fsdp", None),
        P("fsdp"),
        P("fsdp", None),
        P("fsdp", None),
        P("fsdp"),
        P("fsdp", None),
        P("fsdp"),
        P("fsdp"),
        P("fsdp"),
        P("fsdp", None),
        P("fsdp"),
        P("fsdp", None),
        P("fsdp"),
    )
    out_specs = (
        P("fsdp", None),
        P("fsdp", None),
        P("fsdp"),
        P("fsdp"),
        P("fsdp", None),
        P("fsdp"),
        P("fsdp", None),
        P("fsdp", None),
        P("fsdp"),
        P("fsdp", None),
        P("fsdp"),
        P("fsdp"),
        P("fsdp"),
        P("fsdp", None),
        P("fsdp"),
        P("fsdp", None),
        P("fsdp"),
    )
    return jax.shard_map(
        on_device, mesh=mesh, in_specs=in_specs, out_specs=out_specs, check_vma=False
    )
```

```python
import jax
import jax.numpy as jnp
from jax import lax
from jax.experimental import pallas as pl
from jax.experimental.pallas import tpu as pltpu
from jax.sharding import PartitionSpec as P

HD = 64
LENGTH = 128


EPS = 1e-05
BF = jnp.bfloat16
FL = jnp.float32


def normalize(values, gain, shift):
    center = values - jnp.mean(values, -1, keepdims=True)
    spread = jnp.mean(center * center, -1, keepdims=True)
    inverse = lax.rsqrt(spread + EPS)
    plain = center * inverse
    return (plain * gain.astype(FL) + shift.astype(FL), plain, inverse)


def norm_back(grad, plain, inverse, gain):
    scaled = grad * gain.astype(FL)
    inner = (
        scaled
        - jnp.mean(scaled, -1, keepdims=True)
        - plain * jnp.mean(scaled * plain, -1, keepdims=True)
    )
    return (inverse * inner, jnp.sum(grad * plain, 0), jnp.sum(grad, 0))


def project(left, right):
    return jnp.dot(left, right, preferred_element_type=FL)


def back_project(grad, right):
    return jnp.einsum("te,de->td", grad, right, preferred_element_type=FL)


def outer_sum(left, grad):
    return jnp.einsum("td,te->de", left, grad, preferred_element_type=FL)


MESH = pl.DeviceIdType.MESH
LANES = 128
VMEM_BYTES = 50 * 1024 * 1024
OFFSETS = (0, -1, 1, -2, 2, -3, 3)


def place():
    me = lax.axis_index("fsdp")
    z = me // 8
    core = me % 2
    across_x = 2 * (1 - 2 * ((me // 2) % 2))
    across_y = 4 * (1 - 2 * ((me // 4) % 2))
    first = across_x * (1 - core) + across_y * core
    second = across_x * core + across_y * (1 - core)
    return me, z, first, second, 1 - 2 * core


def greet(me, z, first, second, sibling):
    barrier = pltpu.get_barrier_semaphore()

    def signal(device):
        pl.semaphore_signal(barrier, inc=1, device_id=(device,), device_id_type=MESH)

    signal(me + first)
    signal(me + second)
    signal(me + sibling)

    @pl.when(z > 0)
    def _():
        signal(me - 8)

    @pl.when(z < 3)
    def _():
        signal(me + 8)

    pl.semaphore_wait(barrier, 3 + (z + 3) // 4 + (6 - z) // 4)


def gather_kernel(a_ref, b_ref, all_a, all_b, sent, landed, kept):
    me, z, first, second, sibling = place()
    ring = me % 8
    pairs = ((a_ref, all_a), (b_ref, all_b))
    locals_ = [
        pltpu.make_async_copy(own, whole.at[me], kept.at[k]) for k, (own, whole) in enumerate(pairs)
    ]
    for copy in locals_:
        copy.start()
    greet(me, z, first, second, sibling)

    def copies(block, device, slot, own=False, only=(0, 1)):
        return [
            pltpu.make_async_remote_copy(
                src_ref=piece if own else whole.at[block],
                dst_ref=whole.at[block],
                send_sem=sent.at[k, slot],
                recv_sem=landed.at[k, block],
                device_id=(device,),
                device_id_type=MESH,
            )
            for k, (piece, whole) in enumerate(pairs)
            if k in only
        ]

    def send(block, device, slot, own=False, only=(0, 1)):
        for copy in copies(block, device, slot, own, only):
            copy.start()

    def arrive(block, only=(0, 1)):
        for copy in copies(block, me, 0, only=only):
            copy.wait_recv()

    def line(step, offset, finish):
        other = z + offset
        block = me + 8 * offset
        own = offset == 0

        def act(device, slot, k):
            if finish:
                for copy in copies(block, device, slot, own, (k,)):
                    copy.wait_send()
            else:
                send(block, device, slot, own, (k,))

        @pl.when((other >= 0) & (other <= 3))
        def _():
            for k in range(2):
                if not own and not finish:
                    arrive(block, (k,))
                if offset <= 0:

                    @pl.when(z < 3)
                    def _():
                        act(me + 8, 4 * step, k)

                if offset >= 0:

                    @pl.when(z > 0)
                    def _():
                        act(me - 8, 4 * step + 3, k)

                act(me + first, 4 * step + 1, k)
                act(me + second, 4 * step + 2, k)
                act(me + sibling, 28 + step, k)

    def across(step, offset, near, far, finish):
        other = z + offset
        block = me + 8 * offset + near * first + far * second
        base = 35 + 7 * (near + 2 * far - 1)

        @pl.when((other >= 0) & (other <= 3))
        def _():
            for k in range(2):
                if not finish:
                    arrive(block, (k,))
                    if not far:
                        send(block, me + second, 56 + step, only=(k,))
                    send(block, me + sibling, base + step, only=(k,))
                else:
                    for copy in copies(block, me + sibling, base + step, only=(k,)):
                        copy.wait_send()
                    if not far:
                        for copy in copies(block, me + second, 56 + step, only=(k,)):
                            copy.wait_send()

    for finish in (False, True):
        for step in range(len(OFFSETS) + 2):
            if step < len(OFFSETS):
                line(step, OFFSETS[step], finish)
            if 1 <= step <= len(OFFSETS):
                across(step - 1, OFFSETS[step - 1], 1, 0, finish)
                across(step - 1, OFFSETS[step - 1], 0, 1, finish)
            if step >= 2:
                across(step - 2, OFFSETS[step - 2], 1, 1, finish)
    for index in range(16):
        arrive(2 * index + (ring + sibling) % 2)
    for copy in locals_:
        copy.wait()


def gather_blocks(a, b, devices):
    if devices != 32:
        return lax.all_gather(a, "fsdp", axis=0), lax.all_gather(b, "fsdp", axis=0)
    return pl.pallas_call(
        gather_kernel,
        out_shape=(
            jax.ShapeDtypeStruct((devices,) + a.shape, a.dtype),
            jax.ShapeDtypeStruct((devices,) + b.shape, b.dtype),
        ),
        in_specs=[pl.BlockSpec(memory_space=pl.ANY)] * 2,
        out_specs=(pl.BlockSpec(memory_space=pl.ANY),) * 2,
        scratch_shapes=[
            pltpu.SemaphoreType.DMA((2, 64)),
            pltpu.SemaphoreType.DMA((2, 32)),
            pltpu.SemaphoreType.DMA((2,)),
        ],
        compiler_params=pltpu.CompilerParams(
            collective_id=0, has_side_effects=True, vmem_limit_bytes=VMEM_BYTES
        ),
    )(a, b)


def scatter_kernel(
    a_ref,
    b_ref,
    out_a,
    out_b,
    own_a,
    own_b,
    pair_a,
    pair_b,
    two_a,
    two_b,
    one_a,
    one_b,
    line_a,
    line_b,
    sent,
    landed,
    loaded,
):
    me, z, first, second, sibling = place()
    ring = me % 8
    whole = (a_ref, b_ref)
    own, pair = (own_a, own_b), (pair_a, pair_b)
    two, one, lane = (two_a, two_b), (one_a, one_b), (line_a, line_b)
    final = (out_a, out_b)

    def slot16(block):
        return block // 2

    half = z // 2
    goals = (3 - 3 * half, 2 - half, z + 1 - 2 * (z % 2), z)
    kinds = ((1, 1), (0, 1), (1, 0), (0, 0))
    orders = [(to, a, b) for to in goals for a, b in kinds]

    loads = []
    for order, (to, a, b) in enumerate(orders):
        block = 8 * to + ring + a * first + b * second
        for k in range(2):
            copy = pltpu.make_async_copy(
                whole[k].at[block], own[k].at[slot16(block)], loaded.at[k, order]
            )
            copy.start()
            loads.append(copy)
    greet(me, z, first, second, sibling)

    def remote(source, target, k, out_slot, in_slot, device):
        return pltpu.make_async_remote_copy(
            src_ref=source,
            dst_ref=target,
            send_sem=sent.at[k, out_slot],
            recv_sem=landed.at[k, in_slot],
            device_id=(device,),
            device_id_type=MESH,
        )

    def pair_copy(order, to, a, b, k):
        block = 8 * to + (ring + sibling) + b * first + a * second
        return remote(
            whole[k].at[block], pair[k].at[slot16(block)], k, order, slot16(block), me + sibling
        )

    for order, (to, a, b) in enumerate(orders):
        for k in range(2):
            pair_copy(order, to, a, b, k).start()

    def add(k, target, sources):
        if k == 0:
            wide = target.shape[-1]
            chunk = LANES * max(d for d in range(1, 9) if (wide // LANES) % d == 0)

            @pl.loop(0, wide // chunk)
            def _(i):
                part = pl.ds(pl.multiple_of(i * chunk, LANES), chunk)
                total = sources[0][:, part].astype(FL)
                for source in sources[1:]:
                    total = total + source[:, part].astype(FL)
                target[:, part] = total.astype(target.dtype)
        else:
            chunk = 16

            @pl.loop(0, target.shape[0] // chunk)
            def _(i):
                part = pl.ds(pl.multiple_of(i * chunk, chunk), chunk)
                total = sources[0][part, :].astype(FL)
                for source in sources[1:]:
                    total = total + source[part, :].astype(FL)
                target[part, :] = total.astype(target.dtype)

    def base(order, to, a, b, k):
        block = 8 * to + ring + a * first + b * second
        slot = slot16(block)
        loads[2 * order + k].wait()
        remote(whole[k].at[block], pair[k].at[slot], k, 0, slot, me).wait_recv()
        return own[k].at[slot], pair[k].at[slot]

    def second_copy(to, a, k, source):
        return remote(source, two[k].at[2 * to + a], k, 16 + 2 * to + a, 16 + 2 * to + a, me + second)

    def first_copy(to, k, source):
        return remote(source, one[k].at[to], k, 24 + to, 24 + to, me + first)

    def along(goal, k, upward):
        slot = goal + (0 if upward else 4)
        mine = own[k].at[slot16(8 * goal + ring)]
        return remote(
            mine, lane[k].at[slot], k, 28 + slot, 28 + slot, me + 8 if upward else me - 8
        )

    def to_second(step):
        for kind in (0, 1):
            to, a, b = orders[4 * step + kind]
            for k in range(2):
                mine, theirs = base(4 * step + kind, to, a, b, k)
                add(k, mine, (mine, theirs))
                second_copy(to, a, k, mine).start()

    def to_first(step):
        to, a, b = orders[4 * step + 2]
        for k in range(2):
            mine, theirs = base(4 * step + 2, to, a, b, k)
            second_copy(to, a, k, mine).wait_recv()
            add(k, mine, (mine, theirs, two[k].at[2 * to + a]))
            first_copy(to, k, mine).start()

    def to_line(step):
        to, a, b = orders[4 * step + 3]
        for k in range(2):
            mine, theirs = base(4 * step + 3, to, a, b, k)
            second_copy(to, a, k, mine).wait_recv()
            first_copy(to, k, mine).wait_recv()
            sources = (mine, theirs, two[k].at[2 * to + a], one[k].at[to])
            up, down = along(to, k, True), along(to, k, False)
            from_below, from_above = lane[k].at[to], lane[k].at[4 + to]
            if step == 3:

                @pl.when(z == 0)
                def _():
                    down.wait_recv()
                    add(k, final[k], sources + (from_above,))

                @pl.when(z == 3)
                def _():
                    up.wait_recv()
                    add(k, final[k], sources + (from_below,))

                @pl.when((z > 0) & (z < 3))
                def _():
                    up.wait_recv()
                    down.wait_recv()
                    add(k, final[k], sources + (from_below, from_above))

                continue

            @pl.when(to > z)
            def _():
                @pl.when(z > 0)
                def _():
                    up.wait_recv()
                    add(k, mine, sources + (from_below,))

                @pl.when(z == 0)
                def _():
                    add(k, mine, sources)

                up.start()

            @pl.when(to < z)
            def _():
                @pl.when(z < 3)
                def _():
                    down.wait_recv()
                    add(k, mine, sources + (from_above,))

                @pl.when(z == 3)
                def _():
                    add(k, mine, sources)

                down.start()

    to_second(0)
    to_second(1)
    to_second(2)
    to_first(0)
    to_second(3)
    to_first(1)
    to_line(0)
    to_first(2)
    to_line(1)
    to_first(3)
    to_line(2)
    to_line(3)

    for order, (to, a, b) in enumerate(orders):
        for k in range(2):
            pair_copy(order, to, a, b, k).wait_send()
            mine = own[k].at[0]
            if b == 1:
                second_copy(to, a, k, mine).wait_send()
            elif a == 1:
                first_copy(to, k, mine).wait_send()
            elif order < 12:

                @pl.when(to > z)
                def _():
                    along(to, k, True).wait_send()

                @pl.when(to < z)
                def _():
                    along(to, k, False).wait_send()


def scatter_blocks(a, b, devices):
    if devices != 32:
        return (
            lax.psum_scatter(a.astype(FL), "fsdp", scatter_dimension=0),
            lax.psum_scatter(b.astype(FL), "fsdp", scatter_dimension=0),
        )
    vmem = pl.BlockSpec(memory_space=pltpu.VMEM)
    scratch = []
    for count in (16, 16, 8, 4, 8):
        scratch.append(pltpu.VMEM((count,) + a.shape[1:], BF))
        scratch.append(pltpu.VMEM((count,) + b.shape[1:], BF))
    return pl.pallas_call(
        scatter_kernel,
        out_shape=(
            jax.ShapeDtypeStruct(a.shape[1:], FL),
            jax.ShapeDtypeStruct(b.shape[1:], FL),
        ),
        in_specs=[pl.BlockSpec(memory_space=pl.ANY)] * 2,
        out_specs=(vmem, vmem),
        scratch_shapes=scratch
        + [
            pltpu.SemaphoreType.DMA((2, 36)),
            pltpu.SemaphoreType.DMA((2, 36)),
            pltpu.SemaphoreType.DMA((2, 16)),
        ],
        compiler_params=pltpu.CompilerParams(
            collective_id=1, has_side_effects=True, vmem_limit_bytes=VMEM_BYTES
        ),
    )(a, b)


def column_sums(values):
    return jnp.sum(values, 0)


def on_device(
    tokens,
    cotangent,
    counts,
    ln1_gain,
    ln1_bias,
    w_query,
    b_query,
    w_key,
    w_value,
    b_value,
    w_out,
    b_out,
    ln2_gain,
    ln2_bias,
    w_fc1,
    b_fc1,
    w_fc2,
    b_fc2,
):
    devices = lax.axis_size("fsdp")
    rows, width = tokens.shape
    slots = rows // LENGTH
    heads = width // HD
    depth = w_query.shape[0]
    hidden = w_fc1.shape[1]
    wide = 4 * width + hidden

    vectors = (ln1_gain, ln1_bias, b_query, b_value, b_out, ln2_gain, ln2_bias, b_fc2)
    few = len(vectors)
    per_row = b_fc1.shape[0] // depth
    as_rows = depth > few and per_row * depth <= LANES
    if as_rows:
        lines = [jnp.pad(v[None, :], ((0, 0), (0, LANES - depth))) for v in vectors]
        lines.append(jnp.pad(b_fc1[None, :], ((0, 0), (0, LANES - per_row * depth))))
        small = jnp.concatenate(lines, axis=0)
        small = jnp.pad(small, ((0, depth - few - 1), (0, 0)))
    else:
        small = jnp.concatenate([jnp.stack(vectors, 1), b_fc1.reshape(depth, per_row)], axis=1)
        small = jnp.pad(small, ((0, 0), (0, LANES - small.shape[1])))
    block_a = jnp.concatenate([w_query, w_key, w_value, w_out, w_fc1, small], axis=1)
    all_a, all_b = gather_blocks(block_a, w_fc2, devices)
    small = all_a[:, :, wide:]
    all_a = all_a.reshape(width, wide + LANES)
    w_in = all_a[:, : 3 * width]
    w_out = all_a[:, 3 * width : 4 * width]
    w_fc1 = all_a[:, 4 * width : wide]
    w_fc2 = all_b.reshape(hidden, width)
    if as_rows:
        table = small[:, :few, :depth].astype(FL).transpose(1, 0, 2).reshape(few, width)
        b_fc1 = small[:, few, : per_row * depth].astype(FL).reshape(hidden)
    else:
        small = small.reshape(width, LANES).astype(FL)
        table = small[:, :few].T
        b_fc1 = small[:, few : few + per_row].reshape(hidden)
    ln1_gain, ln1_bias, b_query, b_value, b_out, ln2_gain, ln2_bias, b_fc2 = table

    live = (jnp.arange(rows, dtype=jnp.int32) // LENGTH < counts[0]).astype(FL)[:, None]
    inputs = tokens.astype(FL)
    normed_full, plain_one, inverse_one = normalize(inputs, ln1_gain, ln1_bias)
    normed = normed_full.astype(BF)
    b_in = jnp.concatenate([b_query, jnp.zeros_like(b_query), b_value])
    in_rows = (project(normed, w_in) + b_in).astype(BF)

    def split(values):
        return values.reshape(slots, LENGTH, heads, HD)

    queries = split(in_rows[:, :width])
    key_rows = split(in_rows[:, width : 2 * width])
    value_rows = split(in_rows[:, 2 * width :])
    scores = jnp.einsum("bqhd,bkhd->bhqk", queries, key_rows, preferred_element_type=FL)
    scores = scores * HD ** (-0.5)
    causal = jnp.arange(LENGTH)[:, None] >= jnp.arange(LENGTH)[None, :]
    scores = jnp.where(causal, scores, -1e30)
    highest = jnp.max(scores, -1, keepdims=True)
    expo = jnp.exp(scores - highest)
    probs = expo / jnp.sum(expo, -1, keepdims=True)
    weights = probs.astype(BF)
    attended = jnp.einsum("bhqk,bkhd->bqhd", weights, value_rows, preferred_element_type=FL)
    attended = attended.reshape(rows, width).astype(BF)
    middle = inputs + project(attended, w_out) + b_out
    normed_two_full, plain_two, inverse_two = normalize(middle, ln2_gain, ln2_bias)
    normed_two = normed_two_full.astype(BF)
    hidden_pre = project(normed_two, w_fc1) + b_fc1
    gelu, gelu_pull = jax.vjp(jax.nn.gelu, hidden_pre)
    activated = gelu.astype(BF)
    mixed = (live * (middle + project(activated, w_fc2) + b_fc2)).astype(BF)

    grad_out = cotangent.astype(FL) * live
    grad_rows = grad_out.astype(BF)
    grad_w_fc2 = outer_sum(activated, grad_rows)
    grad_act = back_project(grad_rows, w_fc2)
    grad_pre = gelu_pull(grad_act)[0].astype(BF)
    grad_w_fc1 = outer_sum(normed_two, grad_pre)
    grad_norm_two = back_project(grad_pre, w_fc1)
    through_two, grad_ln2_gain, grad_ln2_bias = norm_back(
        grad_norm_two, plain_two, inverse_two, ln2_gain
    )
    grad_middle = grad_out + through_two
    grad_branch = grad_middle.astype(BF)
    grad_w_out = outer_sum(attended, grad_branch)
    grad_att = split(back_project(grad_branch, w_out).astype(BF))
    grad_probs = jnp.einsum("bqhd,bkhd->bhqk", grad_att, value_rows, preferred_element_type=FL)
    grad_values = jnp.einsum("bhqk,bqhd->bkhd", weights, grad_att, preferred_element_type=FL)
    grad_scores = probs * (grad_probs - jnp.sum(probs * grad_probs, -1, keepdims=True))
    grad_scores = grad_scores.astype(BF)
    grad_queries = jnp.einsum("bhqk,bkhd->bqhd", grad_scores, key_rows, preferred_element_type=FL)
    grad_keys = jnp.einsum("bhqk,bqhd->bkhd", grad_scores, queries, preferred_element_type=FL)
    grad_in = jnp.concatenate(
        [
            (grad_queries * HD ** (-0.5)).astype(BF).reshape(rows, width),
            (grad_keys * HD ** (-0.5)).astype(BF).reshape(rows, width),
            grad_values.astype(BF).reshape(rows, width),
        ],
        axis=1,
    )
    grad_w_in = outer_sum(normed, grad_in)
    grad_norm_one = back_project(grad_in, w_in)
    through_one, grad_ln1_gain, grad_ln1_bias = norm_back(
        grad_norm_one, plain_one, inverse_one, ln1_gain
    )
    grad_tokens = grad_middle + through_one

    in_sums = column_sums(grad_in.astype(FL))
    vectors = (
        grad_ln1_gain,
        grad_ln1_bias,
        in_sums[:width],
        in_sums[2 * width :],
        column_sums(grad_branch.astype(FL)),
        grad_ln2_gain,
        grad_ln2_bias,
        column_sums(grad_out),
    )
    pre_sums = column_sums(grad_pre.astype(FL))
    if as_rows:
        table = jnp.stack(vectors, 0).astype(BF).reshape(few, devices, depth).transpose(1, 0, 2)
        table = jnp.pad(table, ((0, 0), (0, depth - few), (0, LANES - depth)))
        line = pre_sums.astype(BF).reshape(devices, 1, per_row * depth)
        line = jnp.pad(line, ((0, 0), (few, depth - few - 1), (0, LANES - per_row * depth)))
        small = (table + line).reshape(width, LANES)
    else:
        small = jnp.concatenate([jnp.stack(vectors, 1), pre_sums.reshape(width, per_row)], axis=1)
        small = jnp.pad(small, ((0, 0), (0, LANES - small.shape[1])))
    sums_a = jnp.concatenate(
        [grad_w_in.astype(BF), grad_w_out.astype(BF), grad_w_fc1.astype(BF), small.astype(BF)],
        axis=1,
    )
    got_a, got_b = scatter_blocks(
        sums_a.reshape(devices, depth, wide + LANES),
        grad_w_fc2.astype(BF).reshape((devices,) + (hidden // devices, width)),
        devices,
    )
    if as_rows:
        columns = tuple(got_a[i, wide : wide + depth] for i in range(few))
        grad_b_fc1 = got_a[few, wide : wide + per_row * depth]
    else:
        small = got_a[:, wide : wide + few + per_row]
        columns = tuple(small[:, i] for i in range(few))
        grad_b_fc1 = small[:, few:].reshape(hidden // devices)
    return (
        mixed,
        grad_tokens,
        columns[0],
        columns[1],
        got_a[:, :width],
        columns[2],
        got_a[:, width : 2 * width],
        got_a[:, 2 * width : 3 * width],
        columns[3],
        got_a[:, 3 * width : 4 * width],
        columns[4],
        columns[5],
        columns[6],
        got_a[:, 4 * width : wide],
        grad_b_fc1,
        got_b,
        columns[7],
    )


def solution(mesh):
    in_specs = (
        P("fsdp", None),
        P("fsdp", None),
        P("fsdp"),
        P("fsdp"),
        P("fsdp"),
        P("fsdp", None),
        P("fsdp"),
        P("fsdp", None),
        P("fsdp", None),
        P("fsdp"),
        P("fsdp", None),
        P("fsdp"),
        P("fsdp"),
        P("fsdp"),
        P("fsdp", None),
        P("fsdp"),
        P("fsdp", None),
        P("fsdp"),
    )
    out_specs = (
        P("fsdp", None),
        P("fsdp", None),
        P("fsdp"),
        P("fsdp"),
        P("fsdp", None),
        P("fsdp"),
        P("fsdp", None),
        P("fsdp", None),
        P("fsdp"),
        P("fsdp", None),
        P("fsdp"),
        P("fsdp"),
        P("fsdp"),
        P("fsdp", None),
        P("fsdp"),
        P("fsdp", None),
        P("fsdp"),
    )
    return jax.shard_map(
        on_device, mesh=mesh, in_specs=in_specs, out_specs=out_specs, check_vma=False
    )
```

```python
import jax
import jax.numpy as jnp
from jax import lax
from jax.experimental import pallas as pl
from jax.experimental.pallas import tpu as pltpu
from jax.sharding import PartitionSpec as P

HD = 64
LENGTH = 128


EPS = 1e-05
BF = jnp.bfloat16
FL = jnp.float32


def normalize(values, gain, shift):
    center = values - jnp.mean(values, -1, keepdims=True)
    spread = jnp.mean(center * center, -1, keepdims=True)
    inverse = lax.rsqrt(spread + EPS)
    plain = center * inverse
    return (plain * gain.astype(FL) + shift.astype(FL), plain, inverse)


def norm_back(grad, plain, inverse, gain):
    scaled = grad * gain.astype(FL)
    inner = (
        scaled
        - jnp.mean(scaled, -1, keepdims=True)
        - plain * jnp.mean(scaled * plain, -1, keepdims=True)
    )
    return (inverse * inner, jnp.sum(grad * plain, 0), jnp.sum(grad, 0))


def project(left, right):
    return jnp.dot(left, right, preferred_element_type=FL)


def back_project(grad, right):
    return jnp.einsum("te,de->td", grad, right, preferred_element_type=FL)


def outer_sum(left, grad):
    return jnp.einsum("td,te->de", left, grad, preferred_element_type=FL)


MESH = pl.DeviceIdType.MESH
LANES = 128
VMEM_BYTES = 50 * 1024 * 1024
OFFSETS = (0, -1, 1, -2, 2, -3, 3)


def place():
    me = lax.axis_index("fsdp")
    z = me // 8
    core = me % 2
    across_x = 2 * (1 - 2 * ((me // 2) % 2))
    across_y = 4 * (1 - 2 * ((me // 4) % 2))
    first = across_x * (1 - core) + across_y * core
    second = across_x * core + across_y * (1 - core)
    return me, z, first, second, 1 - 2 * core


def greet(me, z, first, second, sibling):
    barrier = pltpu.get_barrier_semaphore()

    def signal(device):
        pl.semaphore_signal(barrier, inc=1, device_id=(device,), device_id_type=MESH)

    signal(me + first)
    signal(me + second)
    signal(me + sibling)

    @pl.when(z > 0)
    def _():
        signal(me - 8)

    @pl.when(z < 3)
    def _():
        signal(me + 8)

    pl.semaphore_wait(barrier, 3 + (z + 3) // 4 + (6 - z) // 4)


def gather_kernel(a_ref, b_ref, all_a, all_b, sent, landed, kept):
    me, z, first, second, sibling = place()
    ring = me % 8
    pairs = ((a_ref, all_a), (b_ref, all_b))
    locals_ = [
        pltpu.make_async_copy(own, whole.at[me], kept.at[k]) for k, (own, whole) in enumerate(pairs)
    ]
    for copy in locals_:
        copy.start()
    greet(me, z, first, second, sibling)

    def copies(block, device, slot, own=False, only=(0, 1)):
        return [
            pltpu.make_async_remote_copy(
                src_ref=piece if own else whole.at[block],
                dst_ref=whole.at[block],
                send_sem=sent.at[k, slot],
                recv_sem=landed.at[k, block],
                device_id=(device,),
                device_id_type=MESH,
            )
            for k, (piece, whole) in enumerate(pairs)
            if k in only
        ]

    def send(block, device, slot, own=False, only=(0, 1)):
        for copy in copies(block, device, slot, own, only):
            copy.start()

    def arrive(block, only=(0, 1)):
        for copy in copies(block, me, 0, only=only):
            copy.wait_recv()

    def line(step, offset, finish):
        other = z + offset
        block = me + 8 * offset
        own = offset == 0

        def act(device, slot, k):
            if finish:
                for copy in copies(block, device, slot, own, (k,)):
                    copy.wait_send()
            else:
                send(block, device, slot, own, (k,))

        @pl.when((other >= 0) & (other <= 3))
        def _():
            for k in range(2):
                if not own and not finish:
                    arrive(block, (k,))
                if offset <= 0:

                    @pl.when(z < 3)
                    def _():
                        act(me + 8, 4 * step, k)

                if offset >= 0:

                    @pl.when(z > 0)
                    def _():
                        act(me - 8, 4 * step + 3, k)

                act(me + first, 4 * step + 1, k)
                act(me + second, 4 * step + 2, k)
                act(me + sibling, 28 + step, k)

    def across(step, offset, near, far, finish):
        other = z + offset
        block = me + 8 * offset + near * first + far * second
        base = 35 + 7 * (near + 2 * far - 1)

        @pl.when((other >= 0) & (other <= 3))
        def _():
            for k in range(2):
                if not finish:
                    arrive(block, (k,))
                    if not far:
                        send(block, me + second, 56 + step, only=(k,))
                    send(block, me + sibling, base + step, only=(k,))
                else:
                    for copy in copies(block, me + sibling, base + step, only=(k,)):
                        copy.wait_send()
                    if not far:
                        for copy in copies(block, me + second, 56 + step, only=(k,)):
                            copy.wait_send()

    for finish in (False, True):
        for step in range(len(OFFSETS) + 2):
            if step < len(OFFSETS):
                line(step, OFFSETS[step], finish)
            if 1 <= step <= len(OFFSETS):
                across(step - 1, OFFSETS[step - 1], 1, 0, finish)
                across(step - 1, OFFSETS[step - 1], 0, 1, finish)
            if step >= 2:
                across(step - 2, OFFSETS[step - 2], 1, 1, finish)
    for index in range(16):
        arrive(2 * index + (ring + sibling) % 2)
    for copy in locals_:
        copy.wait()


def gather_blocks(a, b, devices):
    if devices != 32:
        return lax.all_gather(a, "fsdp", axis=0), lax.all_gather(b, "fsdp", axis=0)
    return pl.pallas_call(
        gather_kernel,
        out_shape=(
            jax.ShapeDtypeStruct((devices,) + a.shape, a.dtype),
            jax.ShapeDtypeStruct((devices,) + b.shape, b.dtype),
        ),
        in_specs=[pl.BlockSpec(memory_space=pl.ANY)] * 2,
        out_specs=(pl.BlockSpec(memory_space=pl.ANY),) * 2,
        scratch_shapes=[
            pltpu.SemaphoreType.DMA((2, 64)),
            pltpu.SemaphoreType.DMA((2, 32)),
            pltpu.SemaphoreType.DMA((2,)),
        ],
        compiler_params=pltpu.CompilerParams(
            collective_id=0, has_side_effects=True, vmem_limit_bytes=VMEM_BYTES
        ),
    )(a, b)


def scatter_kernel(
    a_ref,
    b_ref,
    out_a,
    out_b,
    own_a,
    own_b,
    pair_a,
    pair_b,
    two_a,
    two_b,
    one_a,
    one_b,
    line_a,
    line_b,
    sent,
    landed,
    loaded,
):
    me, z, first, second, sibling = place()
    ring = me % 8
    whole = (a_ref, b_ref)
    own, pair = (own_a, own_b), (pair_a, pair_b)
    two, one, lane = (two_a, two_b), (one_a, one_b), (line_a, line_b)
    final = (out_a, out_b)

    def slot16(block):
        return block // 2

    half = z // 2
    goals = (3 - 3 * half, 2 - half, z + 1 - 2 * (z % 2), z)
    kinds = ((1, 1), (0, 1), (1, 0), (0, 0))
    orders = [(to, a, b) for to in goals for a, b in kinds]

    loads = []
    for order, (to, a, b) in enumerate(orders):
        block = 8 * to + ring + a * first + b * second
        for k in range(2):
            copy = pltpu.make_async_copy(
                whole[k].at[block], own[k].at[slot16(block)], loaded.at[k, order]
            )
            copy.start()
            loads.append(copy)
    greet(me, z, first, second, sibling)

    def remote(source, target, k, out_slot, in_slot, device):
        return pltpu.make_async_remote_copy(
            src_ref=source,
            dst_ref=target,
            send_sem=sent.at[k, out_slot],
            recv_sem=landed.at[k, in_slot],
            device_id=(device,),
            device_id_type=MESH,
        )

    def pair_copy(order, to, a, b, k):
        block = 8 * to + (ring + sibling) + b * first + a * second
        return remote(
            whole[k].at[block], pair[k].at[slot16(block)], k, order, slot16(block), me + sibling
        )

    for order, (to, a, b) in enumerate(orders):
        for k in range(2):
            pair_copy(order, to, a, b, k).start()

    def add(k, target, sources):
        if k == 0:
            wide = target.shape[-1]
            chunk = LANES * max(d for d in range(1, 9) if (wide // LANES) % d == 0)

            @pl.loop(0, wide // chunk)
            def _(i):
                part = pl.ds(pl.multiple_of(i * chunk, LANES), chunk)
                total = sources[0][:, part].astype(FL)
                for source in sources[1:]:
                    total = total + source[:, part].astype(FL)
                target[:, part] = total.astype(target.dtype)
        else:
            chunk = 16

            @pl.loop(0, target.shape[0] // chunk)
            def _(i):
                part = pl.ds(pl.multiple_of(i * chunk, chunk), chunk)
                total = sources[0][part, :].astype(FL)
                for source in sources[1:]:
                    total = total + source[part, :].astype(FL)
                target[part, :] = total.astype(target.dtype)

    def base(order, to, a, b, k):
        block = 8 * to + ring + a * first + b * second
        slot = slot16(block)
        loads[2 * order + k].wait()
        remote(whole[k].at[block], pair[k].at[slot], k, 0, slot, me).wait_recv()
        return own[k].at[slot], pair[k].at[slot]

    def second_copy(to, a, k, source):
        return remote(source, two[k].at[2 * to + a], k, 16 + 2 * to + a, 16 + 2 * to + a, me + second)

    def first_copy(to, k, source):
        return remote(source, one[k].at[to], k, 24 + to, 24 + to, me + first)

    def along(goal, k, upward):
        slot = goal + (0 if upward else 4)
        mine = own[k].at[slot16(8 * goal + ring)]
        return remote(
            mine, lane[k].at[slot], k, 28 + slot, 28 + slot, me + 8 if upward else me - 8
        )

    def to_second(step):
        for kind in (0, 1):
            to, a, b = orders[4 * step + kind]
            for k in range(2):
                mine, theirs = base(4 * step + kind, to, a, b, k)
                add(k, mine, (mine, theirs))
                second_copy(to, a, k, mine).start()

    def to_first(step):
        to, a, b = orders[4 * step + 2]
        for k in range(2):
            mine, theirs = base(4 * step + 2, to, a, b, k)
            second_copy(to, a, k, mine).wait_recv()
            add(k, mine, (mine, theirs, two[k].at[2 * to + a]))
            first_copy(to, k, mine).start()

    def to_line(step):
        to, a, b = orders[4 * step + 3]
        for k in range(2):
            mine, theirs = base(4 * step + 3, to, a, b, k)
            second_copy(to, a, k, mine).wait_recv()
            first_copy(to, k, mine).wait_recv()
            sources = (mine, theirs, two[k].at[2 * to + a], one[k].at[to])
            up, down = along(to, k, True), along(to, k, False)
            from_below, from_above = lane[k].at[to], lane[k].at[4 + to]
            if step == 3:

                @pl.when(z == 0)
                def _():
                    down.wait_recv()
                    add(k, final[k], sources + (from_above,))

                @pl.when(z == 3)
                def _():
                    up.wait_recv()
                    add(k, final[k], sources + (from_below,))

                @pl.when((z > 0) & (z < 3))
                def _():
                    up.wait_recv()
                    down.wait_recv()
                    add(k, final[k], sources + (from_below, from_above))

                continue

            @pl.when(to > z)
            def _():
                @pl.when(z > 0)
                def _():
                    up.wait_recv()
                    add(k, mine, sources + (from_below,))

                @pl.when(z == 0)
                def _():
                    add(k, mine, sources)

                up.start()

            @pl.when(to < z)
            def _():
                @pl.when(z < 3)
                def _():
                    down.wait_recv()
                    add(k, mine, sources + (from_above,))

                @pl.when(z == 3)
                def _():
                    add(k, mine, sources)

                down.start()

    to_second(0)
    to_second(1)
    to_second(2)
    to_first(0)
    to_second(3)
    to_first(1)
    to_line(0)
    to_first(2)
    to_line(1)
    to_first(3)
    to_line(2)
    to_line(3)

    for order, (to, a, b) in enumerate(orders):
        for k in range(2):
            pair_copy(order, to, a, b, k).wait_send()
            mine = own[k].at[0]
            if b == 1:
                second_copy(to, a, k, mine).wait_send()
            elif a == 1:
                first_copy(to, k, mine).wait_send()
            elif order < 12:

                @pl.when(to > z)
                def _():
                    along(to, k, True).wait_send()

                @pl.when(to < z)
                def _():
                    along(to, k, False).wait_send()


def scatter_blocks(a, b, devices):
    if devices != 32:
        return (
            lax.psum_scatter(a.astype(FL), "fsdp", scatter_dimension=0),
            lax.psum_scatter(b.astype(FL), "fsdp", scatter_dimension=0),
        )
    vmem = pl.BlockSpec(memory_space=pltpu.VMEM)
    scratch = []
    for count in (16, 16, 8, 4, 8):
        scratch.append(pltpu.VMEM((count,) + a.shape[1:], BF))
        scratch.append(pltpu.VMEM((count,) + b.shape[1:], BF))
    return pl.pallas_call(
        scatter_kernel,
        out_shape=(
            jax.ShapeDtypeStruct(a.shape[1:], FL),
            jax.ShapeDtypeStruct(b.shape[1:], FL),
        ),
        in_specs=[pl.BlockSpec(memory_space=pl.ANY)] * 2,
        out_specs=(vmem, vmem),
        scratch_shapes=scratch
        + [
            pltpu.SemaphoreType.DMA((2, 36)),
            pltpu.SemaphoreType.DMA((2, 36)),
            pltpu.SemaphoreType.DMA((2, 16)),
        ],
        compiler_params=pltpu.CompilerParams(
            collective_id=1, has_side_effects=True, vmem_limit_bytes=VMEM_BYTES
        ),
    )(a, b)


def column_sums(values):
    return jnp.sum(values, 0)


def on_device(
    tokens,
    cotangent,
    counts,
    ln1_gain,
    ln1_bias,
    w_query,
    b_query,
    w_key,
    w_value,
    b_value,
    w_out,
    b_out,
    ln2_gain,
    ln2_bias,
    w_fc1,
    b_fc1,
    w_fc2,
    b_fc2,
):
    devices = lax.axis_size("fsdp")
    rows, width = tokens.shape
    slots = rows // LENGTH
    heads = width // HD
    depth = w_query.shape[0]
    hidden = w_fc1.shape[1]
    wide = 4 * width + hidden

    vectors = (ln1_gain, ln1_bias, b_query, b_value, b_out, ln2_gain, ln2_bias, b_fc2)
    few = len(vectors)
    per_row = b_fc1.shape[0] // depth
    as_rows = depth > few and per_row * depth <= LANES
    if as_rows:
        small = sum(
            jnp.pad(v[None, :], ((i, depth - 1 - i), (0, LANES - v.shape[0])))
            for i, v in enumerate(vectors + (b_fc1,))
        )
    else:
        small = jnp.concatenate([jnp.stack(vectors, 1), b_fc1.reshape(depth, per_row)], axis=1)
        small = jnp.pad(small, ((0, 0), (0, LANES - small.shape[1])))
    pieces = (w_query, w_key, w_value, w_out, w_fc1, small)
    starts = (0, width, 2 * width, 3 * width, 4 * width, wide)
    block_a = sum(
        jnp.pad(piece, ((0, 0), (start, wide + LANES - start - piece.shape[1])))
        for start, piece in zip(starts, pieces)
    )
    all_a, all_b = gather_blocks(block_a, w_fc2, devices)
    small = all_a[:, :, wide:]
    all_a = all_a.reshape(width, wide + LANES)
    w_in = all_a[:, : 3 * width]
    w_out = all_a[:, 3 * width : 4 * width]
    w_fc1 = all_a[:, 4 * width : wide]
    w_fc2 = all_b.reshape(hidden, width)
    if as_rows:
        table = small[:, :few, :depth].astype(FL).transpose(1, 0, 2).reshape(few, width)
        b_fc1 = small[:, few, : per_row * depth].astype(FL).reshape(hidden)
    else:
        small = small.reshape(width, LANES).astype(FL)
        table = small[:, :few].T
        b_fc1 = small[:, few : few + per_row].reshape(hidden)
    ln1_gain, ln1_bias, b_query, b_value, b_out, ln2_gain, ln2_bias, b_fc2 = table

    live = (jnp.arange(rows, dtype=jnp.int32) // LENGTH < counts[0]).astype(FL)[:, None]
    inputs = tokens.astype(FL)
    normed_full, plain_one, inverse_one = normalize(inputs, ln1_gain, ln1_bias)
    normed = normed_full.astype(BF)
    b_in = jnp.concatenate([b_query, jnp.zeros_like(b_query), b_value])
    in_rows = (project(normed, w_in) + b_in).astype(BF)

    def split(values):
        return values.reshape(slots, LENGTH, heads, HD)

    queries = split(in_rows[:, :width])
    key_rows = split(in_rows[:, width : 2 * width])
    value_rows = split(in_rows[:, 2 * width :])
    scores = jnp.einsum("bqhd,bkhd->bhqk", queries, key_rows, preferred_element_type=FL)
    scores = scores * HD ** (-0.5)
    causal = jnp.arange(LENGTH)[:, None] >= jnp.arange(LENGTH)[None, :]
    scores = jnp.where(causal, scores, -1e30)
    highest = jnp.max(scores, -1, keepdims=True)
    expo = jnp.exp(scores - highest)
    probs = expo / jnp.sum(expo, -1, keepdims=True)
    weights = probs.astype(BF)
    attended = jnp.einsum("bhqk,bkhd->bqhd", weights, value_rows, preferred_element_type=FL)
    attended = attended.reshape(rows, width).astype(BF)
    middle = inputs + project(attended, w_out) + b_out
    normed_two_full, plain_two, inverse_two = normalize(middle, ln2_gain, ln2_bias)
    normed_two = normed_two_full.astype(BF)
    hidden_pre = project(normed_two, w_fc1) + b_fc1
    gelu, gelu_pull = jax.vjp(jax.nn.gelu, hidden_pre)
    activated = gelu.astype(BF)
    mixed = (live * (middle + project(activated, w_fc2) + b_fc2)).astype(BF)

    grad_out = cotangent.astype(FL) * live
    grad_rows = grad_out.astype(BF)
    grad_w_fc2 = outer_sum(activated, grad_rows)
    grad_act = back_project(grad_rows, w_fc2)
    grad_pre = gelu_pull(grad_act)[0].astype(BF)
    grad_w_fc1 = outer_sum(normed_two, grad_pre)
    grad_norm_two = back_project(grad_pre, w_fc1)
    through_two, grad_ln2_gain, grad_ln2_bias = norm_back(
        grad_norm_two, plain_two, inverse_two, ln2_gain
    )
    grad_middle = grad_out + through_two
    grad_branch = grad_middle.astype(BF)
    grad_w_out = outer_sum(attended, grad_branch)
    grad_att = split(back_project(grad_branch, w_out).astype(BF))
    grad_probs = jnp.einsum("bqhd,bkhd->bhqk", grad_att, value_rows, preferred_element_type=FL)
    grad_values = jnp.einsum("bhqk,bqhd->bkhd", weights, grad_att, preferred_element_type=FL)
    grad_scores = probs * (grad_probs - jnp.sum(probs * grad_probs, -1, keepdims=True))
    grad_scores = grad_scores.astype(BF)
    grad_queries = jnp.einsum("bhqk,bkhd->bqhd", grad_scores, key_rows, preferred_element_type=FL)
    grad_keys = jnp.einsum("bhqk,bqhd->bkhd", grad_scores, queries, preferred_element_type=FL)
    grad_in = jnp.concatenate(
        [
            (grad_queries * HD ** (-0.5)).astype(BF).reshape(rows, width),
            (grad_keys * HD ** (-0.5)).astype(BF).reshape(rows, width),
            grad_values.astype(BF).reshape(rows, width),
        ],
        axis=1,
    )
    grad_w_in = outer_sum(normed, grad_in)
    grad_norm_one = back_project(grad_in, w_in)
    through_one, grad_ln1_gain, grad_ln1_bias = norm_back(
        grad_norm_one, plain_one, inverse_one, ln1_gain
    )
    grad_tokens = grad_middle + through_one

    in_sums = column_sums(grad_in.astype(FL))
    vectors = (
        grad_ln1_gain,
        grad_ln1_bias,
        in_sums[:width],
        in_sums[2 * width :],
        column_sums(grad_branch.astype(FL)),
        grad_ln2_gain,
        grad_ln2_bias,
        column_sums(grad_out),
    )
    pre_sums = column_sums(grad_pre.astype(FL))
    if as_rows:
        table = lax.optimization_barrier(jnp.stack(vectors, 0))
        table = table.reshape(few, devices, depth).transpose(1, 0, 2).astype(BF)
        table = jnp.pad(table, ((0, 0), (0, depth - few), (0, LANES - depth)))
        line = pre_sums.astype(BF).reshape(devices, 1, per_row * depth)
        line = jnp.pad(line, ((0, 0), (few, depth - few - 1), (0, LANES - per_row * depth)))
        small = (table + line).reshape(width, LANES)
    else:
        small = jnp.concatenate([jnp.stack(vectors, 1), pre_sums.reshape(width, per_row)], axis=1)
        small = jnp.pad(small, ((0, 0), (0, LANES - small.shape[1])))
    sums_a = jnp.concatenate(
        [grad_w_in.astype(BF), grad_w_out.astype(BF), grad_w_fc1.astype(BF), small.astype(BF)],
        axis=1,
    )
    got_a, got_b = scatter_blocks(
        sums_a.reshape(devices, depth, wide + LANES),
        grad_w_fc2.astype(BF).reshape((devices,) + (hidden // devices, width)),
        devices,
    )
    if as_rows:
        columns = tuple(got_a[i, wide : wide + depth] for i in range(few))
        grad_b_fc1 = got_a[few, wide : wide + per_row * depth]
    else:
        small = got_a[:, wide : wide + few + per_row]
        columns = tuple(small[:, i] for i in range(few))
        grad_b_fc1 = small[:, few:].reshape(hidden // devices)
    return (
        mixed,
        grad_tokens,
        columns[0],
        columns[1],
        got_a[:, :width],
        columns[2],
        got_a[:, width : 2 * width],
        got_a[:, 2 * width : 3 * width],
        columns[3],
        got_a[:, 3 * width : 4 * width],
        columns[4],
        columns[5],
        columns[6],
        got_a[:, 4 * width : wide],
        grad_b_fc1,
        got_b,
        columns[7],
    )


def solution(mesh):
    in_specs = (
        P("fsdp", None),
        P("fsdp", None),
        P("fsdp"),
        P("fsdp"),
        P("fsdp"),
        P("fsdp", None),
        P("fsdp"),
        P("fsdp", None),
        P("fsdp", None),
        P("fsdp"),
        P("fsdp", None),
        P("fsdp"),
        P("fsdp"),
        P("fsdp"),
        P("fsdp", None),
        P("fsdp"),
        P("fsdp", None),
        P("fsdp"),
    )
    out_specs = (
        P("fsdp", None),
        P("fsdp", None),
        P("fsdp"),
        P("fsdp"),
        P("fsdp", None),
        P("fsdp"),
        P("fsdp", None),
        P("fsdp", None),
        P("fsdp"),
        P("fsdp", None),
        P("fsdp"),
        P("fsdp"),
        P("fsdp"),
        P("fsdp", None),
        P("fsdp"),
        P("fsdp", None),
        P("fsdp"),
    )
    return jax.shard_map(
        on_device, mesh=mesh, in_specs=in_specs, out_specs=out_specs, check_vma=False
    )
```
